128 devices in a mesh: section: 8 (over x, core), tp: 16 (over z, y).
Axes of the slice: x: 4, y: 4, z: 4, core: 2. Of those that a mesh axis runs over, the one named last changes fastest.
Arguments:
- x_in: bfloat16 [256, 6144], P(None, 'tp'), may hold values from -6 to 6
- cotangent: bfloat16 [256, 6144], P(None, 'tp'), may hold values from -6 to 6
- weights: bfloat16 [8, 6144, 6144], P('section', None, 'tp'), may hold values from -0.0390625 to 0.0390625
- down_weight_store: bfloat16 [8, 8, 6144, 128], P('section', None, 'tp'), may hold values from -0.078125 to 0.078125
- lib_b: bfloat16 [8, 8, 128, 6144], P('section', None, None, 'tp'), may hold values from -0.5 to 0.5
- style_ids: int32 [2, 4], replicated, may hold values from 0 to 7
- slot_of: int32 [8], replicated, may hold values from 0 to 7, each once
Outputs:
- grad_a: bfloat16 [8, 8, 6144, 128], P(None, 'section', 'tp')
- grad_b: bfloat16 [8, 8, 128, 6144], P(None, 'section', None, 'tp')
The draws below stay inside these ranges and needn't reach their ends.
Inputs may be any that keep to these rules, and one draw needn't show every extreme that they name: Each slot once; style k's adapters are stored at slot slot_of[k].
All inputs are finite; a program needn't handle non-finite values.
Results may differ from the reference program's by a relative error of at most 0.035.
Values may be sent and summed in bfloat16 or wider, within the bound.
No kernel may reach another device: no remote copies, remote signals or barrier semaphores. Data moves between devices by JAX's collectives and lax.ppermute only.
A program may use at most 64 MiB of HBM per device.

```python
import math
import jax
import jax.numpy as jnp
import numpy as np
from jax import lax

MODEL_WIDTH = 6144
ADAPTER_RANK = 128
MB = 2
BLOCK = 32
NBLK = 4
TOTAL_ROWS = 256
LAYERS = 8
STYLES = 8
N_TP = 16


def with_ends(entries, own_key, least, largest):
    longest = entries.shape.index(max(entries.shape))
    spots = []
    for shift in (0, 1):
        where = [jax.random.randint(jax.random.fold_in(own_key, axis), (), 0, length) for axis, length in enumerate(entries.shape)]
        where[longest] = (where[longest] + shift) % entries.shape[longest]
        spots.append(tuple(where))
    return entries.at[spots[0]].set(least).at[spots[1]].set(largest)


def shard_levels(own_key, shape, split, smallest, high):
    loudness = 1.0
    for position, parts in split:
        heights = jax.random.uniform(jax.random.fold_in(jax.random.fold_in(own_key, 6), position), (parts,), jnp.float32, smallest / len(split), high / len(split))
        loudness = loudness * jnp.repeat(jnp.exp(heights), shape[position] // parts).reshape((-1,) + (1,) * (len(shape) - 1 - position))
    return loudness


def rank_table(number_of, skew):
    portions = [(1 << 20) // math.isqrt(rank ** skew) + 1 for rank in range(1, number_of + 1)]
    scale = 1 + sum(portions) // (1 << 30)
    return np.cumsum(np.array([max(1, weight // scale) for weight in portions]))


def skewed_ids(own_key, extent, amount, skew):
    grid = rank_table(amount, skew)
    ticket = jax.random.randint(jax.random.fold_in(own_key, 1), extent, 0, int(grid[amount - 1]))
    grade = jnp.searchsorted(jnp.asarray(grid, jnp.int32), ticket, side="right")
    return jax.random.permutation(jax.random.fold_in(own_key, 2), amount)[grade].astype(jnp.int32)


def normal_values(own_key, shape, width, bound, shards=(), held_as=jnp.bfloat16):
    result = jax.random.normal(own_key, shape, jnp.float32) * width
    if len(shards) > 0:
        result = shard_levels(own_key, shape, shards, -0.22, 0.18) * result
    return jnp.clip(result, min=-bound, max=bound).astype(held_as)


def setup_inputs(seed: int = 0) -> dict:
    splits = jax.random.split(jax.random.key(seed), 8)
    return {
        "x_in": normal_values(splits[0], (TOTAL_ROWS, MODEL_WIDTH), 1.0, 6.0, ((1, 16),)),
        "cotangent": normal_values(splits[1], (TOTAL_ROWS, MODEL_WIDTH), 1.0, 6.0, ((1, 16),)),
        "weights": normal_values(splits[2], (LAYERS, MODEL_WIDTH, MODEL_WIDTH), (4 * MODEL_WIDTH) ** -0.5, 0.0390625, ((0, 8), (2, 16))),
        "down_weight_store": normal_values(splits[3], (STYLES, LAYERS, MODEL_WIDTH, ADAPTER_RANK), MODEL_WIDTH ** -0.5, 0.078125, ((0, 8), (2, 16))),
        "lib_b": normal_values(splits[4], (STYLES, LAYERS, ADAPTER_RANK, MODEL_WIDTH), ADAPTER_RANK ** -0.5, 0.5, ((0, 8), (3, 16))),
        "style_ids": with_ends(skewed_ids(splits[5], (MB, NBLK), STYLES, 1), jax.random.fold_in(splits[5], 3), 0, STYLES - 1).astype(jnp.int32),
        "slot_of": jax.random.permutation(splits[6], STYLES).astype(jnp.int32),
    }


ADAPTER_SCALE = 0.25

def partial_sum_round(partial_sums, axis_pos):
    held_bf = lax.optimization_barrier(partial_sums.astype(jnp.bfloat16))
    return lax.optimization_barrier(jnp.sum(held_bf.astype(jnp.float32), axis=axis_pos))

def reference(x_in, cotangent, weights, down_weight_store, lib_b, style_ids, slot_of):
    blocks_overall = MB * NBLK
    feature_columns = MODEL_WIDTH // N_TP
    flat_ids = style_ids.reshape(blocks_overall)
    slot_ids = slot_of[flat_ids]
    owners_of = (flat_ids[None, :] == jnp.arange(STYLES)[:, None]).astype(jnp.float32)
    hidden_state = x_in
    layer_in = []
    layer_pre = []
    layer_hidden = []
    for layer_index in range(LAYERS):
        selected_down_weight = down_weight_store[slot_ids, layer_index].astype(jnp.float32)
        selected_up_weight = lib_b[slot_ids, layer_index].astype(jnp.float32)
        row_blocks = hidden_state.reshape(blocks_overall, BLOCK, N_TP, feature_columns).astype(jnp.float32)
        partial_sums = jnp.einsum('nbpi,npir->npbr', row_blocks, selected_down_weight.reshape(blocks_overall, N_TP, feature_columns, ADAPTER_RANK))
        adapter_hidden = partial_sum_round(partial_sums, 1).astype(jnp.bfloat16)
        raised_rows = jnp.einsum('swz,sze->swe', adapter_hidden.astype(jnp.float32), selected_up_weight).reshape(TOTAL_ROWS, MODEL_WIDTH)
        preactivation = jnp.dot(hidden_state, weights[layer_index], preferred_element_type=jnp.float32) + ADAPTER_SCALE * raised_rows
        layer_in.append(hidden_state)
        layer_pre.append(preactivation)
        layer_hidden.append(adapter_hidden)
        hidden_state = (hidden_state.astype(jnp.float32) + jax.nn.gelu(preactivation)).astype(jnp.bfloat16)
    earlier_neighbour = cotangent
    grads_a = [None] * LAYERS
    grads_b = [None] * LAYERS
    for layer_index in reversed(range(LAYERS)):
        selected_down_weight = down_weight_store[slot_ids, layer_index].astype(jnp.float32)
        selected_up_weight = lib_b[slot_ids, layer_index].astype(jnp.float32)
        gelu_out, gelu_pull = jax.vjp(jax.nn.gelu, layer_pre[layer_index])
        grad_pre = gelu_pull(earlier_neighbour.astype(jnp.float32))[0].astype(jnp.bfloat16)
        gradient_rows = grad_pre.reshape(blocks_overall, BLOCK, N_TP, feature_columns).astype(jnp.float32)
        hidden_rows = layer_hidden[layer_index].reshape(blocks_overall, BLOCK, ADAPTER_RANK).astype(jnp.float32)
        block_up_weight = ADAPTER_SCALE * jnp.einsum('ysk,ysou->ykou', hidden_rows, gradient_rows).reshape(blocks_overall, ADAPTER_RANK, MODEL_WIDTH)
        hidden_pieces = ADAPTER_SCALE * jnp.einsum('ozut,ojut->ouzj', gradient_rows, selected_up_weight.reshape(blocks_overall, ADAPTER_RANK, N_TP, feature_columns))
        backward_hidden = partial_sum_round(hidden_pieces, 1).astype(jnp.bfloat16)
        x_parts = jnp.einsum('rpi,dpi->prd', grad_pre.reshape(TOTAL_ROWS, N_TP, feature_columns).astype(jnp.float32), weights[layer_index].reshape(MODEL_WIDTH, N_TP, feature_columns).astype(jnp.float32))
        backward_input = partial_sum_round(x_parts, 0)
        x_rows = layer_in[layer_index].reshape(blocks_overall, BLOCK, MODEL_WIDTH).astype(jnp.float32)
        block_down_weight = jnp.einsum('nbi,nbr->nir', x_rows, backward_hidden.astype(jnp.float32))
        adapter_input = jnp.einsum('qwa,qla->qwl', backward_hidden.astype(jnp.float32), selected_down_weight).reshape(TOTAL_ROWS, MODEL_WIDTH)
        earlier_neighbour = (earlier_neighbour.astype(jnp.float32) + backward_input + adapter_input).astype(jnp.bfloat16)
        grads_a[layer_index] = jnp.einsum('kn,nir->kir', owners_of, block_down_weight, precision=lax.Precision.HIGHEST).astype(jnp.bfloat16)
        grads_b[layer_index] = jnp.einsum('kn,nri->kri', owners_of, block_up_weight, precision=lax.Precision.HIGHEST).astype(jnp.bfloat16)
    return (jnp.stack(grads_a, axis=1), jnp.stack(grads_b, axis=1))
```

```python
import functools

import jax
import jax.numpy as jnp
from jax import lax
from jax.experimental import pallas as pl
from jax.experimental.pallas import tpu as pltpu
from jax.sharding import PartitionSpec as P

ADAPTER_SCALE = 0.25
SIDE = 4
LAYERS = 8
BLOCKS = 8
ROWS = 32
RANK = 128
CHUNK = 384
WIDE = SIDE * CHUNK
Z_AT = WIDE
OWN_AT = WIDE + RANK
PAY = OWN_AT + CHUNK
PAY_EXTRA = PAY + RANK + CHUNK
BF = jnp.bfloat16
F32 = jnp.float32


def along_a(k):
    return lambda x, c, z, y: (x, c, z, y + k) if c == 0 else (x, c, z + k, y)


def along_b(k):
    return lambda x, c, z, y: (x, c, z + k, y) if c == 0 else (x, c, z, y + k)


def onward(k):
    return lambda x, c, z, y: (x, 1, z, y + k) if c == 0 else (x + 1, 0, z + k, y)


def backward(k):
    return lambda x, c, z, y: (x, 0, z + k, y) if c == 1 else (x - 1, 1, z, y + k)


def send(value, target):
    pairs = []
    for sec in range(2 * SIDE):
        for tp in range(SIDE * SIDE):
            x, c, z, y = target(sec // 2, sec % 2, tp // SIDE, tp % SIDE)
            sec_to = (x % SIDE) * 2 + c
            tp_to = (z % SIDE) * SIDE + y % SIDE
            pairs.append((sec * SIDE * SIDE + tp, sec_to * SIDE * SIDE + tp_to))
    return lax.ppermute(value, ("section", "tp"), pairs)


def chunk_at(index):
    return pl.ds(pl.multiple_of(index * CHUNK, CHUNK), CHUNK)


def dot(left, right):
    return jnp.dot(left, right, preferred_element_type=F32)


def dot_nt(left, right):
    return lax.dot_general(left, right, (((1,), (1,)), ((), ())), preferred_element_type=F32)


def dot_tn(left, right):
    return lax.dot_general(left, right, (((0,), (0,)), ((), ())), preferred_element_type=F32)


def gelu_both(y):
    scale = 0.7978845608028654
    square = y * y
    t = jnp.tanh(scale * y * (1.0 + 0.044715 * square))
    half = 0.5 * (1.0 + t)
    slope = half + 0.5 * y * (1.0 - t * t) * scale * (1.0 + 3.0 * 0.044715 * square)
    return y * half, slope


def forward_kernel(tick, sc, p0, p1, p2, p3, xg, w, a0, a1, a2, a3, b0, b1, b2, b3,
                   _g, _z, _h, pay, g_out, z_out, h_out, h_all):
    at = tick * 8
    first, a, b = sc[at + 3], sc[at + 4], sc[at + 5]
    step = pl.program_id(0)

    @pl.when(step == 0)
    def _():
        z = sum(p[:, Z_AT:OWN_AT].astype(F32) for p in (p0, p1, p2, p3)).astype(BF)
        z_out[0] = z
        z_part = jnp.zeros((ROWS, RANK), F32)
        for k, (p, ak, bk) in enumerate(((p0, a0, b0), (p1, a1, b1), (p2, a2, b2), (p3, a3, b3))):
            here = chunk_at(lax.rem(b - k + SIDE, SIDE))
            y = sum(q[:, here].astype(F32) for q in (p0, p1, p2, p3))
            y = y + ADAPTER_SCALE * dot(z, bk[0])
            value, slope = gelu_both(y)
            h = (p[:, OWN_AT:PAY].astype(F32) + value).astype(BF)
            h = jnp.where(first > 0, xg[:, here], h)
            h_all[:, here] = h
            g_out[0, :, here] = slope
            z_part = z_part + dot(h, ak[0])
            if k == 0:
                h_out[0] = h
                pay[:, OWN_AT:PAY] = h
        pay[:, Z_AT:OWN_AT] = z_part.astype(BF)

    pay[:, chunk_at(lax.rem(a - step + SIDE, SIDE))] = dot(h_all[...], w[0]).astype(BF)


def backward_kernel(tick, sc, q0, q1, q2, q3, cg, w, a0, a1, a2, a3, b0, b1, b2, b3, slope, z_in,
                    _q, _z, _e, pay0, pay, q_out, z_out, e_out, e_all, total):
    at = tick * 8
    first, b = sc[at + 3], sc[at + 5]
    step = pl.program_id(0)

    @pl.when(step == 0)
    def _():
        q = sum(p[:, Z_AT:OWN_AT].astype(F32) for p in (q0, q1, q2, q3)).astype(BF)
        q_out[0] = q
        z_out[0] = q0[:, PAY:PAY + RANK]
        e_out[0] = q0[:, PAY + RANK:]
        q_part = jnp.zeros((ROWS, RANK), F32)
        for k, (p, ak, bk) in enumerate(((q0, a0, b0), (q1, a1, b1), (q2, a2, b2), (q3, a3, b3))):
            here = chunk_at(lax.rem(b - k + SIDE, SIDE))
            n = sum(r[:, here].astype(F32) for r in (q0, q1, q2, q3))
            g = (p[:, OWN_AT:PAY].astype(F32) + n + dot_nt(q, ak[0])).astype(BF)
            g = jnp.where(first > 0, cg[:, here], g)
            e = (slope[0, :, here] * g.astype(F32)).astype(BF)
            e_all[k] = e
            q_part = q_part + dot_nt(e, bk[0])
            if k == 0:
                pay[:, OWN_AT:PAY] = g
                pay0[:, OWN_AT:PAY] = g
                pay0[:, PAY + RANK:] = e
        q_part = (ADAPTER_SCALE * q_part).astype(BF)
        pay[:, Z_AT:OWN_AT] = q_part
        pay0[:, Z_AT:OWN_AT] = q_part
        pay0[:, PAY:PAY + RANK] = z_in[0]
        total[...] = jnp.zeros_like(total)

    total[...] += dot_nt(e_all[step], w[0])

    @pl.when(step == SIDE - 1)
    def _():
        n = total[...].astype(BF)
        pay[:, :WIDE] = n
        pay0[:, :WIDE] = n


def gradient_kernel(sc, x, h, q, z, e, ga, gb):
    style = pl.program_id(0)
    block = lax.broadcasted_iota(jnp.int32, (BLOCKS * ROWS, 1), 0) // ROWS
    mine = jnp.zeros((BLOCKS * ROWS, 1), F32)
    for n in range(BLOCKS):
        mine = jnp.where((block == n) & (sc[n] == style), 1.0, mine)
    rows = jnp.where(sc[BLOCKS] == 0, x[...], h[...])
    q_mine = (q[...].astype(F32) * mine).astype(BF)
    z_mine = (z[...].astype(F32) * mine).astype(BF)
    ga[0, 0] = dot_tn(rows, q_mine).astype(BF)
    gb[0, 0] = (ADAPTER_SCALE * dot_tn(z_mine, e[...])).astype(BF)


def whole(shape):
    return pl.BlockSpec(shape, lambda i, sc: (0,) * len(shape))


def adapter_specs(at, shape):
    return [pl.BlockSpec((1,) + shape, lambda i, sc: (sc[at], 0, 0)) for _ in range(SIDE)]


def slot_spec(at, columns):
    return pl.BlockSpec((1, ROWS, columns), lambda i, sc: (sc[at], 0, 0))


PARAMS = pltpu.CompilerParams(vmem_limit_bytes=24 << 20)


def forward_tick(tick, table, payloads, xg, w, a_lib, b_lib, g_buf, z_buf, h_buf):
    at = tick * 8
    keep = pl.BlockSpec(memory_space=pl.ANY)
    grid_spec = pltpu.PrefetchScalarGridSpec(
        num_scalar_prefetch=1,
        grid=(SIDE,),
        in_specs=[whole((ROWS, PAY))] * SIDE
        + [pl.BlockSpec((ROWS, WIDE), lambda i, sc: (sc[at + 1], 0))]
        + [pl.BlockSpec((1, WIDE, CHUNK), lambda i, sc: (i, 0, 0))]
        + adapter_specs(at, (CHUNK, RANK))
        + adapter_specs(at, (RANK, CHUNK))
        + [keep] * 3,
        out_specs=[whole((ROWS, PAY)), slot_spec(at + 2, WIDE), slot_spec(at + 2, RANK), slot_spec(at + 2, CHUNK)],
        scratch_shapes=[pltpu.VMEM((ROWS, WIDE), BF)],
    )
    like = lambda v: jax.ShapeDtypeStruct(v.shape, v.dtype)
    return pl.pallas_call(
        functools.partial(forward_kernel, tick),
        grid_spec=grid_spec,
        out_shape=[jax.ShapeDtypeStruct((ROWS, PAY), BF), like(g_buf), like(z_buf), like(h_buf)],
        input_output_aliases={15: 1, 16: 2, 17: 3},
        compiler_params=PARAMS,
        name="forward_stage",
    )(table, *payloads, xg, w, *a_lib, *b_lib, g_buf, z_buf, h_buf)


def backward_tick(tick, table, payloads, cg, w, a_lib, b_lib, g_buf, z_buf, q_buf, zr_buf, e_buf):
    at = tick * 8
    keep = pl.BlockSpec(memory_space=pl.ANY)
    grid_spec = pltpu.PrefetchScalarGridSpec(
        num_scalar_prefetch=1,
        grid=(SIDE,),
        in_specs=[whole((ROWS, PAY_EXTRA))] + [whole((ROWS, PAY))] * (SIDE - 1)
        + [pl.BlockSpec((ROWS, WIDE), lambda i, sc: (sc[at + 1] + BLOCKS, 0))]
        + [pl.BlockSpec((1, WIDE, CHUNK), lambda i, sc: (i, 0, 0))]
        + adapter_specs(at, (CHUNK, RANK))
        + adapter_specs(at, (RANK, CHUNK))
        + [slot_spec(at + 1, WIDE), slot_spec(at + 1, RANK)]
        + [keep] * 3,
        out_specs=[whole((ROWS, PAY_EXTRA)), whole((ROWS, PAY)),
                   slot_spec(at + 2, RANK), slot_spec(at + 2, RANK), slot_spec(at + 2, CHUNK)],
        scratch_shapes=[pltpu.VMEM((SIDE, ROWS, CHUNK), BF), pltpu.VMEM((ROWS, WIDE), F32)],
    )
    like = lambda v: jax.ShapeDtypeStruct(v.shape, v.dtype)
    return pl.pallas_call(
        functools.partial(backward_kernel, tick),
        grid_spec=grid_spec,
        out_shape=[jax.ShapeDtypeStruct((ROWS, PAY_EXTRA), BF), jax.ShapeDtypeStruct((ROWS, PAY), BF),
                   like(q_buf), like(zr_buf), like(e_buf)],
        input_output_aliases={17: 2, 18: 3, 19: 4},
        compiler_params=PARAMS,
        name="backward_stage",
    )(table, *payloads, cg, w, *a_lib, *b_lib, g_buf, z_buf, q_buf, zr_buf, e_buf)


def gradients(info, x_in, h_buf, q_buf, zr_buf, e_buf):
    flat = lambda v: v.reshape(-1, v.shape[-1])
    total = BLOCKS * ROWS
    grid_spec = pltpu.PrefetchScalarGridSpec(
        num_scalar_prefetch=1,
        grid=(LAYERS,),
        in_specs=[whole((total, CHUNK)), whole((total, CHUNK)), whole((total, RANK)), whole((total, RANK)),
                  whole((total, CHUNK))],
        out_specs=[pl.BlockSpec((1, 1, CHUNK, RANK), lambda i, sc: (i, 0, 0, 0)),
                   pl.BlockSpec((1, 1, RANK, CHUNK), lambda i, sc: (i, 0, 0, 0))],
    )
    return pl.pallas_call(
        gradient_kernel,
        grid_spec=grid_spec,
        out_shape=[jax.ShapeDtypeStruct((LAYERS, 1, CHUNK, RANK), BF),
                   jax.ShapeDtypeStruct((LAYERS, 1, RANK, CHUNK), BF)],
        compiler_params=PARAMS,
        name="style_gradients",
    )(info, x_in, flat(h_buf), flat(q_buf), flat(zr_buf), flat(e_buf))


def tick_tables(section, slots, a, b):
    def table(ticks, mb, save, first):
        cols = [slots[jnp.clip(mb, 0, BLOCKS - 1)], jnp.clip(mb, 0, BLOCKS - 1),
                jnp.where((save >= 0) & (save < BLOCKS), save, BLOCKS), first.astype(jnp.int32),
                jnp.broadcast_to(a, ticks.shape), jnp.broadcast_to(b, ticks.shape),
                jnp.zeros_like(ticks), jnp.zeros_like(ticks)]
        return jnp.stack(cols, axis=1).astype(jnp.int32).reshape(-1)

    ticks = jnp.arange(2 * LAYERS + BLOCKS, dtype=jnp.int32)
    start = section == 0
    boundary = jnp.where(start, LAYERS, section)
    fwd_mb = ticks - jnp.where(start & (ticks >= LAYERS), LAYERS, section)
    fwd = table(ticks, fwd_mb, ticks - boundary, start & (ticks < LAYERS))
    bwd = table(ticks, ticks - 2 * LAYERS + boundary, ticks - 2 * LAYERS + section,
                jnp.broadcast_to(start, ticks.shape))
    return fwd, bwd


def body(x_in, cotangent, weights, down_weight_store, lib_b, style_ids, slot_of):
    section = lax.axis_index("section")
    tp = lax.axis_index("tp")
    core, z_pos, y_pos = section % 2, tp // SIDE, tp % SIDE
    a = jnp.where(core == 0, y_pos, z_pos)
    b = jnp.where(core == 0, z_pos, y_pos)
    flat_ids = style_ids.reshape(-1)
    styles = jnp.arange(slot_of.shape[0], dtype=jnp.int32)
    slots = jnp.sum(jnp.where(flat_ids[:, None] == styles[None, :], slot_of[None, :], 0), axis=1)
    fwd_table, bwd_table = tick_tables(section, slots, a, b)

    with jax.named_scope("weight_blocks"):
        grid4 = weights[0].reshape(SIDE, SIDE, CHUNK, CHUNK)
        pieces = []
        for k in range(SIDE):
            to = lax.rem(a + k, SIDE)
            for_core0 = lax.dynamic_slice_in_dim(grid4, to, 1, 1).reshape(WIDE, CHUNK)
            for_core1 = lax.dynamic_slice_in_dim(grid4, to, 1, 0).reshape(WIDE, CHUNK)
            pieces.append(jnp.where(core == 0, for_core0, for_core1))
        w_own = jnp.stack([pieces[0]] + [send(pieces[k], along_a(k)) for k in range(1, SIDE)])
        w_prev = send(w_own, onward(0))
    with jax.named_scope("ends"):
        ends = jnp.concatenate([x_in, cotangent], axis=0)
        ends_all = jnp.zeros((ends.shape[0], WIDE), BF)
        for k in range(SIDE):
            piece = ends if k == 0 else send(ends, along_b(k))
            ends_all = lax.dynamic_update_slice(ends_all, piece, (0, lax.rem(b - k + SIDE, SIDE) * CHUNK))
    with jax.named_scope("adapters"):
        a_own = lax.all_to_all(down_weight_store, "section", split_axis=1, concat_axis=0, tiled=True)[:, 0]
        b_own = lax.all_to_all(lib_b, "section", split_axis=1, concat_axis=0, tiled=True)[:, 0]
        a_lib = [a_own] + [send(a_own, along_b(k)) for k in range(1, SIDE)]
        b_lib = [send(b_own, onward(k)) for k in range(SIDE)]

    fwd_in = [jnp.zeros((ROWS, PAY), BF)] * SIDE
    bwd_in = [jnp.zeros((ROWS, PAY_EXTRA), BF)] + [jnp.zeros((ROWS, PAY), BF)] * (SIDE - 1)
    buffer = lambda columns, dtype: jnp.zeros((BLOCKS + 1, ROWS, columns), dtype)
    g_buf, z_buf, h_buf = buffer(WIDE, F32), buffer(RANK, BF), buffer(CHUNK, BF)
    q_buf, zr_buf, e_buf = buffer(RANK, BF), buffer(RANK, BF), buffer(CHUNK, BF)
    for tick in range(2 * LAYERS + BLOCKS):
        if tick < LAYERS + BLOCKS:
            with jax.named_scope("forward"):
                pay, g_buf, z_buf, h_buf = forward_tick(
                    tick, fwd_table, fwd_in, ends_all, w_own, a_lib, b_lib, g_buf, z_buf, h_buf)
                if tick < LAYERS + BLOCKS - 1:
                    fwd_in = [send(pay, onward(k)) for k in range(SIDE)]
        if tick >= LAYERS:
            with jax.named_scope("backward"):
                pay0, pay, q_buf, zr_buf, e_buf = backward_tick(
                    tick, bwd_table, bwd_in, ends_all, w_prev, a_lib, b_lib, g_buf, z_buf, q_buf, zr_buf, e_buf)
                if tick < 2 * LAYERS + BLOCKS - 1:
                    bwd_in = [send(pay0, backward(0))] + [send(pay, backward(k)) for k in range(1, SIDE)]
    info = jnp.concatenate([flat_ids, section[None]]).astype(jnp.int32)
    with jax.named_scope("gradients"):
        grad_a, grad_b = gradients(info, x_in, h_buf, q_buf, zr_buf, e_buf)
    return grad_a, grad_b


def solution(mesh):
    in_specs = (
        P(None, "tp"),
        P(None, "tp"),
        P("section", None, "tp"),
        P("section", None, "tp", None),
        P("section", None, None, "tp"),
        P(),
        P(),
    )
    out_specs = (P(None, "section", "tp", None), P(None, "section", None, "tp"))
    return jax.shard_map(body, mesh=mesh, in_specs=in_specs, out_specs=out_specs, check_vma=False)
```

```python
import functools

import jax
import jax.numpy as jnp
from jax import lax
from jax.experimental import pallas as pl
from jax.experimental.pallas import tpu as pltpu
from jax.sharding import PartitionSpec as P

ADAPTER_SCALE = 0.25
SIDE = 4
LAYERS = 8
BLOCKS = 8
ROWS = 32
TOKENS = BLOCKS * ROWS
RANK = 128
CHUNK = 384
WIDE = SIDE * CHUNK
PAIR = 2 * RANK
Z_AT = WIDE
OWN_AT = WIDE + RANK
PAY = OWN_AT + CHUNK
PAY_EXTRA = PAY + RANK + CHUNK
BF = jnp.bfloat16
F32 = jnp.float32


def along_a(k):
    return lambda x, c, z, y: (x, c, z, y + k) if c == 0 else (x, c, z + k, y)


def along_b(k):
    return lambda x, c, z, y: (x, c, z + k, y) if c == 0 else (x, c, z, y + k)


def onward(k):
    return lambda x, c, z, y: (x, 1, z, y + k) if c == 0 else (x + 1, 0, z + k, y)


def backward(k):
    return lambda x, c, z, y: (x, 0, z + k, y) if c == 1 else (x - 1, 1, z, y + k)


def send(value, target):
    pairs = []
    for sec in range(2 * SIDE):
        for tp in range(SIDE * SIDE):
            x, c, z, y = target(sec // 2, sec % 2, tp // SIDE, tp % SIDE)
            sec_to = (x % SIDE) * 2 + c
            tp_to = (z % SIDE) * SIDE + y % SIDE
            pairs.append((sec * SIDE * SIDE + tp, sec_to * SIDE * SIDE + tp_to))
    return lax.ppermute(value, ("section", "tp"), pairs)


IN_VMEM = pl.BlockSpec(memory_space=pltpu.VMEM)
IN_SMEM = pl.BlockSpec(memory_space=pltpu.SMEM)
ANYWHERE = pl.BlockSpec(memory_space=pl.ANY)
PARAMS = pltpu.CompilerParams(vmem_limit_bytes=24 << 20)


def shaped(*shape, dtype=BF):
    return jax.ShapeDtypeStruct(shape, dtype)


def chunk_at(index):
    return pl.ds(pl.multiple_of(index * CHUNK, CHUNK), CHUNK)


def dot(left, right):
    return jnp.dot(left, right, preferred_element_type=F32)


def dot_nt(left, right):
    return lax.dot_general(left, right, (((1,), (1,)), ((), ())), preferred_element_type=F32)


def dot_tn(left, right):
    return lax.dot_general(left, right, (((0,), (0,)), ((), ())), preferred_element_type=F32)


def gelu_both(y):
    scale = 0.7978845608028654
    square = y * y
    t = jnp.tanh(scale * y * (1.0 + 0.044715 * square))
    half = 0.5 * (1.0 + t)
    slope = half + 0.5 * y * (1.0 - t * t) * scale * (1.0 + 3.0 * 0.044715 * square)
    return y * half, slope


def run_copies(moves, sems):
    copies = [pltpu.make_async_copy(source, target, sems.at[i]) for i, (source, target) in enumerate(moves)]
    for copy in copies:
        copy.start()
    for copy in copies:
        copy.wait()


def copy_kernel(name, kernel, count, out_shape, out_spec, scalars, *operands):
    many = isinstance(out_shape, list)
    return pl.pallas_call(
        kernel,
        in_specs=[IN_SMEM] + [ANYWHERE] * len(operands),
        out_specs=[out_spec] * len(out_shape) if many else out_spec,
        out_shape=out_shape,
        scratch_shapes=[pltpu.SemaphoreType.DMA((count,))],
        compiler_params=PARAMS,
        name=name,
    )(scalars, *operands)


def pack_layers_kernel(a, b, out):
    out[0, :RANK] = a[0, 0].T
    out[0, RANK:] = b[0, 0]


def pack_layers(a, b):
    return pl.pallas_call(
        pack_layers_kernel,
        grid=(LAYERS,),
        in_specs=[pl.BlockSpec((1, 1, CHUNK, RANK), lambda i: (0, i, 0, 0)),
                  pl.BlockSpec((1, 1, RANK, CHUNK), lambda i: (0, lax.rem(i + LAYERS - 1, LAYERS), 0, 0))],
        out_specs=pl.BlockSpec((1, PAIR, CHUNK), lambda i: (i, 0, 0)),
        out_shape=shaped(LAYERS, PAIR, CHUNK),
        compiler_params=PARAMS,
        name="pack_layers",
    )(a, b)


def cut_weights_kernel(sc, w, o0, o1, o2, o3, sems):
    core, a = sc[0], sc[2]
    moves = []
    for k, out in enumerate((o0, o1, o2, o3)):
        to = lax.rem(a + k, SIDE)
        for j in range(SIDE):
            source = jnp.where(core == 0, j * SIDE + to, to * SIDE + j)
            moves.append((w.at[source], out.at[j]))
    run_copies(moves, sems)


def pack_blocks_kernel(sc, x, cot, ab, out, sems):
    moves = [(x, out.at[pl.ds(0, TOKENS)]), (cot, out.at[pl.ds(TOKENS, TOKENS)])]
    for n in range(BLOCKS):
        moves.append((ab.at[sc[8 + n]], out.at[pl.ds(2 * TOKENS + n * PAIR, PAIR)]))
    run_copies(moves, sems)


def settle_weights_kernel(sc, own, w1, w2, w3, out, sems):
    copies = [pltpu.make_async_copy(w, out.at[k + 1], sems.at[k]) for k, w in enumerate((w1, w2, w3))]
    for copy in copies:
        copy.start()
    out[0] = own[...]
    for copy in copies:
        copy.wait()


def settle_weights(scalars, pieces):
    return pl.pallas_call(
        settle_weights_kernel,
        in_specs=[IN_SMEM, IN_VMEM] + [ANYWHERE] * (SIDE - 1),
        out_specs=IN_VMEM,
        out_shape=shaped(SIDE, WIDE, CHUNK),
        scratch_shapes=[pltpu.SemaphoreType.DMA((SIDE - 1,))],
        compiler_params=PARAMS,
        name="settle_weights",
    )(scalars, *pieces)


def settle_blocks_kernel(sc, own, p1, p2, p3, x, cot, ab, sems):
    parts = [(0, x), (TOKENS, cot)]
    copies = []
    for k, piece in enumerate((p1, p2, p3)):
        for i, (start, out) in enumerate(parts):
            copies.append(pltpu.make_async_copy(piece.at[pl.ds(start, TOKENS)], out.at[k + 1], sems.at[k, i]))
        copies.append(pltpu.make_async_copy(piece.at[pl.ds(2 * TOKENS, BLOCKS * PAIR)], ab.at[k + 1], sems.at[k, 2]))
    for copy in copies:
        copy.start()
    for start, out in parts:
        out[0] = own[pl.ds(start, TOKENS)]
    ab[0] = own[pl.ds(2 * TOKENS, BLOCKS * PAIR)]
    for copy in copies:
        copy.wait()


def settle_blocks(scalars, pieces):
    return pl.pallas_call(
        settle_blocks_kernel,
        in_specs=[IN_SMEM, IN_VMEM] + [ANYWHERE] * (SIDE - 1),
        out_specs=[IN_VMEM] * 3,
        out_shape=[shaped(SIDE, TOKENS, CHUNK), shaped(SIDE, TOKENS, CHUNK), shaped(SIDE, BLOCKS * PAIR, CHUNK)],
        scratch_shapes=[pltpu.SemaphoreType.DMA((SIDE - 1, 3))],
        compiler_params=PARAMS,
        name="settle_blocks",
    )(scalars, *pieces)


def settle_previous_kernel(sc, w, out, sems):
    run_copies([(w.at[k], out.at[k]) for k in range(SIDE)], sems)


def transpose_kernel(w, out):
    out[0] = w[0].T


def transposed(w):
    return pl.pallas_call(
        transpose_kernel,
        grid=(SIDE,),
        in_specs=[pl.BlockSpec((1, WIDE, CHUNK), lambda i: (i, 0, 0))],
        out_specs=pl.BlockSpec((1, CHUNK, WIDE), lambda i: (i, 0, 0)),
        out_shape=shaped(SIDE, CHUNK, WIDE),
        compiler_params=PARAMS,
        name="transpose_weights",
    )(w)


def within(index):
    return jnp.clip(index, 0, BLOCKS - 1)


def slot_or_spare(index):
    return jnp.where((index >= 0) & (index < BLOCKS), index, BLOCKS)


def forward_block(tick, section):
    return within(tick - jnp.where((section == 0) & (tick >= LAYERS), LAYERS, section))


def boundary(section):
    return jnp.where(section == 0, LAYERS, section)


def forward_save(tick, section):
    return slot_or_spare(tick - boundary(section))


def backward_block(tick, section):
    return within(tick - 2 * LAYERS + boundary(section))


def backward_save(tick, section):
    return slot_or_spare(tick - 2 * LAYERS + section)


def forward_kernel(tick, sc, p0, p1, p2, p3, rows, w, ab, _g, _z, _h, pay, g_out, z_out, h_out, h_all):
    section, a, b = sc[1], sc[2], sc[3]
    block = forward_block(tick, section)
    own_rows = pl.ds(pl.multiple_of(block * ROWS, ROWS), ROWS)
    down = pl.ds(pl.multiple_of(block * PAIR, PAIR), RANK)
    up = pl.ds(pl.multiple_of(block * PAIR + RANK, RANK), RANK)
    z = sum(p[:, Z_AT:OWN_AT].astype(F32) for p in (p0, p1, p2, p3)).astype(BF)
    z_out[0] = z
    z_part = jnp.zeros((ROWS, RANK), F32)
    for k, p in enumerate((p0, p1, p2, p3)):
        here = chunk_at(lax.rem(b - k + SIDE, SIDE))
        y = sum(q[:, here].astype(F32) for q in (p0, p1, p2, p3))
        value, slope = gelu_both(y + ADAPTER_SCALE * dot(z, ab[k, up]))
        h = (p[:, OWN_AT:PAY].astype(F32) + value).astype(BF)
        if tick < LAYERS:
            h = jnp.where(section == 0, rows[k, own_rows], h)
        h_all[:, here] = h
        g_out[0, :, here] = slope
        z_part = z_part + dot_nt(h, ab[k, down])
        if k == 0:
            h_out[0] = h
            pay[:, OWN_AT:PAY] = h
    pay[:, Z_AT:OWN_AT] = z_part.astype(BF)
    h = h_all[...]
    for k in range(SIDE):
        pay[:, chunk_at(lax.rem(a - k + SIDE, SIDE))] = dot(h, w[k]).astype(BF)


def backward_kernel(tick, sc, q0, q1, q2, q3, rows, wt, ab, slope, z_in,
                    _q, _z, _e, pay0, pay, q_out, z_out, e_out):
    section, b = sc[1], sc[3]
    block = backward_block(tick, section)
    q = sum(p[:, Z_AT:OWN_AT].astype(F32) for p in (q0, q1, q2, q3)).astype(BF)
    q_out[0] = q
    z_out[0] = q0[:, PAY:PAY + RANK]
    e_out[0] = q0[:, PAY + RANK:]
    q_part = jnp.zeros((ROWS, RANK), F32)
    total = jnp.zeros((ROWS, WIDE), F32)
    own_rows = pl.ds(pl.multiple_of(block * ROWS, ROWS), ROWS)
    down = pl.ds(pl.multiple_of(block * PAIR, PAIR), RANK)
    up = pl.ds(pl.multiple_of(block * PAIR + RANK, RANK), RANK)
    for k, p in enumerate((q0, q1, q2, q3)):
        here = chunk_at(lax.rem(b - k + SIDE, SIDE))
        n = sum(r[:, here].astype(F32) for r in (q0, q1, q2, q3))
        g = (p[:, OWN_AT:PAY].astype(F32) + n + dot(q, ab[k, down])).astype(BF)
        g = jnp.where(section == 0, rows[k, own_rows], g)
        e = (slope[0, :, here] * g.astype(F32)).astype(BF)
        q_part = q_part + dot_nt(e, ab[k, up])
        total = total + dot(e, wt[k])
        if k == 0:
            pay[:, OWN_AT:PAY] = g
            pay0[:, OWN_AT:PAY] = g
            pay0[:, PAY + RANK:] = e
    q_part = (ADAPTER_SCALE * q_part).astype(BF)
    pay[:, Z_AT:OWN_AT] = q_part
    pay0[:, Z_AT:OWN_AT] = q_part
    pay0[:, PAY:PAY + RANK] = z_in[0]
    n = total.astype(BF)
    pay[:, :WIDE] = n
    pay0[:, :WIDE] = n


def gradient_kernel(sc, x, h, q, z, e, ga, gb):
    style = pl.program_id(0)
    block = lax.broadcasted_iota(jnp.int32, (TOKENS, 1), 0) // ROWS
    mine = jnp.zeros((TOKENS, 1), F32)
    for n in range(BLOCKS):
        mine = jnp.where((block == n) & (sc[16 + n] == style), 1.0, mine)
    rows = jnp.where(sc[1] == 0, x[...], h[...])
    q_mine = (q[...].astype(F32) * mine).astype(BF)
    z_mine = (z[...].astype(F32) * mine).astype(BF)
    ga[0, 0] = dot_tn(rows, q_mine).astype(BF)
    gb[0, 0] = (ADAPTER_SCALE * dot_tn(z_mine, e[...])).astype(BF)


def slot_spec(slot, tick, columns):
    return pl.BlockSpec((1, ROWS, columns), lambda i, sc: (slot(tick, sc[1]), 0, 0))


def forward_tick(tick, scalars, payloads, rows, w, ab, g_buf, z_buf, h_buf):
    grid_spec = pltpu.PrefetchScalarGridSpec(
        num_scalar_prefetch=1,
        grid=(1,),
        in_specs=[IN_VMEM] * 7 + [ANYWHERE] * 3,
        out_specs=[IN_VMEM] + [slot_spec(forward_save, tick, columns) for columns in (WIDE, RANK, CHUNK)],
        scratch_shapes=[pltpu.VMEM((ROWS, WIDE), BF)],
    )
    return pl.pallas_call(
        functools.partial(forward_kernel, tick),
        grid_spec=grid_spec,
        out_shape=[shaped(ROWS, PAY)] + [shaped(*v.shape, dtype=v.dtype) for v in (g_buf, z_buf, h_buf)],
        input_output_aliases={8: 1, 9: 2, 10: 3},
        compiler_params=PARAMS,
        name="forward_stage",
    )(scalars, *payloads, rows, w, ab, g_buf, z_buf, h_buf)


def backward_tick(tick, scalars, payloads, rows, wt, ab, g_buf, z_buf, q_buf, zr_buf, e_buf):
    grid_spec = pltpu.PrefetchScalarGridSpec(
        num_scalar_prefetch=1,
        grid=(1,),
        in_specs=[IN_VMEM] * 7 + [slot_spec(backward_block, tick, columns) for columns in (WIDE, RANK)]
        + [ANYWHERE] * 3,
        out_specs=[IN_VMEM] * 2 + [slot_spec(backward_save, tick, columns) for columns in (RANK, RANK, CHUNK)],
    )
    return pl.pallas_call(
        functools.partial(backward_kernel, tick),
        grid_spec=grid_spec,
        out_shape=[shaped(ROWS, PAY_EXTRA), shaped(ROWS, PAY)]
        + [shaped(*v.shape, dtype=v.dtype) for v in (q_buf, zr_buf, e_buf)],
        input_output_aliases={10: 2, 11: 3, 12: 4},
        compiler_params=PARAMS,
        name="backward_stage",
    )(scalars, *payloads, rows, wt, ab, g_buf, z_buf, q_buf, zr_buf, e_buf)


def gradients(scalars, x_in, h_buf, q_buf, zr_buf, e_buf):
    flat = lambda v: v.reshape(-1, v.shape[-1])
    whole = lambda columns: pl.BlockSpec((TOKENS, columns), lambda i, sc: (0, 0))
    grid_spec = pltpu.PrefetchScalarGridSpec(
        num_scalar_prefetch=1,
        grid=(LAYERS,),
        in_specs=[whole(CHUNK), whole(CHUNK), whole(RANK), whole(RANK), whole(CHUNK)],
        out_specs=[pl.BlockSpec((1, 1, CHUNK, RANK), lambda i, sc: (i, 0, 0, 0)),
                   pl.BlockSpec((1, 1, RANK, CHUNK), lambda i, sc: (i, 0, 0, 0))],
    )
    return pl.pallas_call(
        gradient_kernel,
        grid_spec=grid_spec,
        out_shape=[shaped(LAYERS, 1, CHUNK, RANK), shaped(LAYERS, 1, RANK, CHUNK)],
        compiler_params=PARAMS,
        name="style_gradients",
    )(scalars, x_in, flat(h_buf), flat(q_buf), flat(zr_buf), flat(e_buf))


def body(x_in, cotangent, weights, down_weight_store, lib_b, style_ids, slot_of):
    section = lax.axis_index("section")
    tp = lax.axis_index("tp")
    core, z_pos, y_pos = section % 2, tp // SIDE, tp % SIDE
    a = jnp.where(core == 0, y_pos, z_pos)
    b = jnp.where(core == 0, z_pos, y_pos)
    flat_ids = style_ids.reshape(-1)
    styles = jnp.arange(slot_of.shape[0], dtype=jnp.int32)
    slots = jnp.sum(jnp.where(flat_ids[:, None] == styles[None, :], slot_of[None, :], 0), axis=1)
    place = jnp.stack([core, section, a, b, 0, 0, 0, 0]).astype(jnp.int32)
    scalars = jnp.concatenate([place, slots, flat_ids])

    with jax.named_scope("adapters"):
        ab_out = pack_layers(down_weight_store, lib_b)
        ab_in = lax.all_to_all(ab_out, "section", split_axis=0, concat_axis=0, tiled=True)
    with jax.named_scope("weight_blocks"):
        cut = copy_kernel("cut_weights", cut_weights_kernel, SIDE * SIDE, [shaped(SIDE, CHUNK, CHUNK)] * SIDE, ANYWHERE,
                          place, weights[0].reshape(SIDE * SIDE, CHUNK, CHUNK))
        cut = [piece.reshape(WIDE, CHUNK) for piece in cut]
        w_pieces = [cut[0]] + [send(cut[k], along_a(k)) for k in range(1, SIDE)]
    with jax.named_scope("blocks"):
        packed = copy_kernel("pack_blocks", pack_blocks_kernel, 2 + BLOCKS, shaped(2 * TOKENS + BLOCKS * PAIR, CHUNK),
                             ANYWHERE, scalars, x_in, cotangent, ab_in)
        block_pieces = [packed] + [send(packed, along_b(k)) for k in range(1, SIDE)]
    with jax.named_scope("weight_blocks"):
        w_pieces[0], _ = lax.optimization_barrier((w_pieces[0], packed))
        w_own = settle_weights(place, w_pieces)
        w_turned = transposed(w_own)
    with jax.named_scope("previous_weights"):
        w_prev = send(w_turned, onward(0))
    with jax.named_scope("blocks"):
        block_pieces[0], _ = lax.optimization_barrier((block_pieces[0], w_turned))
        x_rows, cot_rows, ab = settle_blocks(place, block_pieces)

    first_in = jnp.zeros((ROWS, PAY), BF)
    fwd_in = [first_in] * SIDE
    bwd_in = [jnp.zeros((ROWS, PAY_EXTRA), BF)] + [jnp.zeros((ROWS, PAY), BF)] * (SIDE - 1)
    buffer = lambda columns, dtype: jnp.zeros((BLOCKS + 1, ROWS, columns), dtype)
    g_buf, z_buf, h_buf = buffer(WIDE, F32), buffer(RANK, BF), buffer(CHUNK, BF)
    q_buf, zr_buf, e_buf = buffer(RANK, BF), buffer(RANK, BF), buffer(CHUNK, BF)
    for tick in range(2 * LAYERS + BLOCKS):
        if tick == 4:
            with jax.named_scope("previous_weights"):
                w_prev, fwd_in[0] = lax.optimization_barrier((w_prev, fwd_in[0]))
                w_prev = copy_kernel("settle_previous", settle_previous_kernel, SIDE, shaped(SIDE, CHUNK, WIDE),
                                     IN_VMEM, place, w_prev)
        if tick < LAYERS + BLOCKS:
            with jax.named_scope("forward"):
                pay, g_buf, z_buf, h_buf = forward_tick(
                    tick, place, fwd_in, x_rows, w_own, ab, g_buf, z_buf, h_buf)
                if tick < LAYERS + BLOCKS - 1:
                    fwd_in = [send(pay, onward(k)) for k in range(SIDE)]
        if tick >= LAYERS:
            with jax.named_scope("backward"):
                pay0, pay, q_buf, zr_buf, e_buf = backward_tick(
                    tick, place, bwd_in, cot_rows, w_prev, ab, g_buf, z_buf, q_buf, zr_buf, e_buf)
                if tick < 2 * LAYERS + BLOCKS - 1:
                    bwd_in = [send(pay0, backward(0))] + [send(pay, backward(k)) for k in range(1, SIDE)]
    with jax.named_scope("gradients"):
        grad_a, grad_b = gradients(scalars, x_in, h_buf, q_buf, zr_buf, e_buf)
    return grad_a, grad_b


def solution(mesh):
    in_specs = (
        P(None, "tp"),
        P(None, "tp"),
        P("section", None, "tp"),
        P("section", None, "tp", None),
        P("section", None, None, "tp"),
        P(),
        P(),
    )
    out_specs = (P(None, "section", "tp", None), P(None, "section", None, "tp"))
    return jax.shard_map(body, mesh=mesh, in_specs=in_specs, out_specs=out_specs, check_vma=False)
```

```python
import functools

import jax
import jax.numpy as jnp
from jax import lax
from jax.experimental import pallas as pl
from jax.experimental.pallas import tpu as pltpu
from jax.sharding import PartitionSpec as P

ADAPTER_SCALE = 0.25
SIDE = 4
LAYERS = 8
BLOCKS = 8
ROWS = 32
TOKENS = BLOCKS * ROWS
RANK = 128
CHUNK = 384
WIDE = SIDE * CHUNK
PARTS = CHUNK // RANK
PAIR = 2 * RANK
PACKED = 2 * TOKENS + BLOCKS * PAIR
LAST_FORWARD = LAYERS + BLOCKS - 1
LAST_BACKWARD = 2 * LAYERS + BLOCKS - 1
Z_AT = WIDE
OWN_AT = WIDE + RANK
PAY = OWN_AT + CHUNK
PAY_EXTRA = PAY + RANK + CHUNK
STYLES_AT_ONCE = 4
BF = jnp.bfloat16
F32 = jnp.float32


def along_a(k):
    return lambda x, c, z, y: (x, c, z, y + k) if c == 0 else (x, c, z + k, y)


def along_b(k):
    return lambda x, c, z, y: (x, c, z + k, y) if c == 0 else (x, c, z, y + k)


def onward(k):
    return lambda x, c, z, y: (x, 1, z, y + k) if c == 0 else (x + 1, 0, z + k, y)


def backward(k):
    return lambda x, c, z, y: (x, 0, z + k, y) if c == 1 else (x - 1, 1, z, y + k)


def send(value, target):
    pairs = []
    for sec in range(2 * SIDE):
        for tp in range(SIDE * SIDE):
            x, c, z, y = target(sec // 2, sec % 2, tp // SIDE, tp % SIDE)
            sec_to = (x % SIDE) * 2 + c
            tp_to = (z % SIDE) * SIDE + y % SIDE
            pairs.append((sec * SIDE * SIDE + tp, sec_to * SIDE * SIDE + tp_to))
    return lax.ppermute(value, ("section", "tp"), pairs)


IN_VMEM = pl.BlockSpec(memory_space=pltpu.VMEM)
IN_SMEM = pl.BlockSpec(memory_space=pltpu.SMEM)
ANYWHERE = pl.BlockSpec(memory_space=pl.ANY)
SMALL = pl.CostEstimate(flops=0, bytes_accessed=1024, transcendentals=0)
PARAMS = pltpu.CompilerParams(vmem_limit_bytes=16 << 20)


def shaped(*shape, dtype=BF):
    return jax.ShapeDtypeStruct(shape, dtype)


def chunk_at(index):
    return pl.ds(pl.multiple_of(index * CHUNK, CHUNK), CHUNK)


def dot(left, right):
    return jnp.dot(left, right, preferred_element_type=F32)


def dot_nt(left, right):
    return lax.dot_general(left, right, (((1,), (1,)), ((), ())), preferred_element_type=F32)


def dot_tn(left, right):
    return lax.dot_general(left, right, (((0,), (0,)), ((), ())), preferred_element_type=F32)


def parts(value):
    return [value[:, part * RANK:(part + 1) * RANK] for part in range(PARTS)]


def gelu_both(y):
    scale = 0.7978845608028654
    square = y * y
    t = jnp.tanh(scale * y * (1.0 + 0.044715 * square))
    half = 0.5 * (1.0 + t)
    slope = half + 0.5 * y * (1.0 - t * t) * scale * (1.0 + 3.0 * 0.044715 * square)
    return y * half, slope


def run_copies(moves, sems):
    copies = [pltpu.make_async_copy(source, target, sems.at[i]) for i, (source, target) in enumerate(moves)]
    for copy in copies:
        copy.start()
    for copy in copies:
        copy.wait()


def copy_kernel(name, kernel, count, out_shape, out_spec, scalars, *operands):
    many = isinstance(out_shape, list)
    return pl.pallas_call(
        kernel,
        in_specs=[IN_SMEM] + [ANYWHERE] * len(operands),
        out_specs=[out_spec] * len(out_shape) if many else out_spec,
        out_shape=out_shape,
        scratch_shapes=[pltpu.SemaphoreType.DMA((count,))],
        compiler_params=PARAMS,
        cost_estimate=SMALL,
        name=name,
    )(scalars, *operands)


def pack_layers_kernel(a, b, out):
    for layer in range(LAYERS):
        for part in range(PARTS):
            out[layer, :RANK, part * RANK:(part + 1) * RANK] = a[0, layer, part * RANK:(part + 1) * RANK]
        out[layer, RANK:] = b[0, (layer - 1) % LAYERS]


def pack_layers(a, b):
    return pl.pallas_call(
        pack_layers_kernel,
        in_specs=[IN_VMEM] * 2,
        out_specs=IN_VMEM,
        out_shape=shaped(LAYERS, PAIR, CHUNK),
        compiler_params=PARAMS,
        name="pack_layers",
    )(a, b)


def cut_weights_kernel(sc, w, o0, o1, o2, o3, sems):
    core, a = sc[0], sc[2]
    moves = []
    for k, out in enumerate((o0, o1, o2, o3)):
        to = lax.rem(a + k, SIDE)
        for j in range(SIDE):
            source = jnp.where(core == 0, j * SIDE + to, to * SIDE + j)
            moves.append((w.at[source], out.at[j]))
    run_copies(moves, sems)


def pack_blocks_kernel(sc, x, cot, ab, out, sems):
    moves = [(x, out.at[pl.ds(0, TOKENS)]), (cot, out.at[pl.ds(TOKENS, TOKENS)])]
    for n in range(BLOCKS):
        moves.append((ab.at[sc[8 + n]], out.at[pl.ds(2 * TOKENS + n * PAIR, PAIR)]))
    run_copies(moves, sems)


def settle_weights_kernel(sc, own, w1, w2, w3, out, sems):
    copies = [pltpu.make_async_copy(w, out.at[k + 1], sems.at[k]) for k, w in enumerate((w1, w2, w3))]
    for copy in copies:
        copy.start()
    out[0] = own[...]
    for copy in copies:
        copy.wait()


def settle_weights(scalars, pieces):
    return pl.pallas_call(
        settle_weights_kernel,
        in_specs=[IN_SMEM, IN_VMEM] + [ANYWHERE] * (SIDE - 1),
        out_specs=IN_VMEM,
        out_shape=shaped(SIDE, WIDE, CHUNK),
        scratch_shapes=[pltpu.SemaphoreType.DMA((SIDE - 1,))],
        compiler_params=PARAMS,
        cost_estimate=SMALL,
        name="settle_weights",
    )(scalars, *pieces)


def settle_blocks_kernel(sc, own, p1, p2_first, p2_second, p3, x, cot, ab, sems):
    head = 2 * TOKENS
    split = PACKED // 2 - head
    moves = []
    for k, piece in ((1, p1), (2, p2_first), (3, p3)):
        count = split if k == 2 else BLOCKS * PAIR
        moves.append((piece.at[pl.ds(0, TOKENS)], x.at[k]))
        moves.append((piece.at[pl.ds(TOKENS, TOKENS)], cot.at[k]))
        moves.append((piece.at[pl.ds(head, count)], ab.at[k, pl.ds(0, count)]))
    moves.append((p2_second, ab.at[2, pl.ds(split, PACKED // 2)]))
    copies = [pltpu.make_async_copy(source, target, sems.at[i]) for i, (source, target) in enumerate(moves)]
    for copy in copies:
        copy.start()
    x[0] = own[pl.ds(0, TOKENS)]
    cot[0] = own[pl.ds(TOKENS, TOKENS)]
    ab[0] = own[pl.ds(head, BLOCKS * PAIR)]
    for copy in copies:
        copy.wait()


def settle_blocks(scalars, pieces):
    return pl.pallas_call(
        settle_blocks_kernel,
        in_specs=[IN_SMEM, IN_VMEM] + [ANYWHERE] * SIDE,
        out_specs=[IN_VMEM] * 3,
        out_shape=[shaped(SIDE, TOKENS, CHUNK), shaped(SIDE, TOKENS, CHUNK), shaped(SIDE, BLOCKS * PAIR, CHUNK)],
        scratch_shapes=[pltpu.SemaphoreType.DMA((10,))],
        compiler_params=PARAMS,
        cost_estimate=SMALL,
        name="settle_blocks",
    )(scalars, *pieces)


def settle_previous_kernel(sc, w, out, sems):
    run_copies([(w.at[k], out.at[k]) for k in range(SIDE)], sems)


def transpose_kernel(w, out):
    out[0] = w[0].T


def transposed(w):
    return pl.pallas_call(
        transpose_kernel,
        grid=(SIDE,),
        in_specs=[pl.BlockSpec((1, WIDE, CHUNK), lambda i: (i, 0, 0))],
        out_specs=pl.BlockSpec((1, CHUNK, WIDE), lambda i: (i, 0, 0)),
        out_shape=shaped(SIDE, CHUNK, WIDE),
        compiler_params=PARAMS,
        cost_estimate=SMALL,
        name="transpose_weights",
    )(w)


def within(index):
    return jnp.clip(index, 0, BLOCKS - 1)


def slot_or_spare(index):
    return jnp.where((index >= 0) & (index < BLOCKS), index, BLOCKS)


def forward_block(tick, section):
    return within(tick - jnp.where((section == 0) & (tick >= LAYERS), LAYERS, section))


def boundary(section):
    return jnp.where(section == 0, LAYERS, section)


def forward_save(tick, section):
    return slot_or_spare(tick - boundary(section))


def backward_block(tick, section):
    return within(tick - 2 * LAYERS + boundary(section))


def backward_save(tick, section):
    return slot_or_spare(tick - 2 * LAYERS + section)


def forward_kernel(tick, sc, p0, p1, p2, p3, rows, w, ab, _g, _z, _h, pay, g_out, z_out, h_out, h_all):
    section, a, b = sc[1], sc[2], sc[3]
    block = forward_block(tick, section)
    own_rows = pl.ds(pl.multiple_of(block * ROWS, ROWS), ROWS)
    down = pl.ds(pl.multiple_of(block * PAIR, PAIR), RANK)
    up = pl.ds(pl.multiple_of(block * PAIR + RANK, RANK), RANK)
    z = sum(p[:, Z_AT:OWN_AT].astype(F32) for p in (p0, p1, p2, p3)).astype(BF)
    z_out[0] = z
    z_part = jnp.zeros((ROWS, RANK), F32)
    for k, p in enumerate((p0, p1, p2, p3)):
        here = chunk_at(lax.rem(b - k + SIDE, SIDE))
        y = sum(q[:, here].astype(F32) for q in (p0, p1, p2, p3))
        value, slope = gelu_both(y + ADAPTER_SCALE * dot(z, ab[k, up]))
        h = (p[:, OWN_AT:PAY].astype(F32) + value).astype(BF)
        if tick < LAYERS:
            h = jnp.where(section == 0, rows[k, own_rows], h)
        h_all[:, here] = h
        g_out[0, :, here] = slope
        if tick < LAST_FORWARD:
            for piece, weight in zip(parts(h), parts(ab[k, down])):
                z_part = z_part + dot(piece, weight)
        if k == 0:
            h_out[0] = h
            pay[:, OWN_AT:PAY] = h
    pay[:, Z_AT:OWN_AT] = z_part.astype(BF)
    if tick == LAST_FORWARD:
        return
    h = h_all[...]
    for k in range(SIDE):
        pay[:, chunk_at(lax.rem(a - k + SIDE, SIDE))] = dot(h, w[k]).astype(BF)


def backward_kernel(tick, sc, q0, q1, q2, q3, rows, wt, ab, slope, z_in,
                    _q, _z, _e, pay0, pay, q_out, z_out, e_out):
    section, b = sc[1], sc[3]
    block = backward_block(tick, section)
    q = sum(p[:, Z_AT:OWN_AT].astype(F32) for p in (q0, q1, q2, q3)).astype(BF)
    q_out[0] = q
    z_out[0] = q0[:, PAY:PAY + RANK]
    e_out[0] = q0[:, PAY + RANK:]
    if tick == LAST_BACKWARD:
        return
    q_part = jnp.zeros((ROWS, RANK), F32)
    total = jnp.zeros((ROWS, WIDE), F32)
    own_rows = pl.ds(pl.multiple_of(block * ROWS, ROWS), ROWS)
    down = pl.ds(pl.multiple_of(block * PAIR, PAIR), RANK)
    up = pl.ds(pl.multiple_of(block * PAIR + RANK, RANK), RANK)
    for k, p in enumerate((q0, q1, q2, q3)):
        here = chunk_at(lax.rem(b - k + SIDE, SIDE))
        n = sum(r[:, here].astype(F32) for r in (q0, q1, q2, q3))
        back = jnp.concatenate([dot_nt(q, weight) for weight in parts(ab[k, down])], axis=1)
        g = (p[:, OWN_AT:PAY].astype(F32) + n + back).astype(BF)
        g = jnp.where(section == 0, rows[k, own_rows], g)
        e = (slope[0, :, here] * g.astype(F32)).astype(BF)
        q_part = q_part + dot_nt(e, ab[k, up])
        total = total + dot(e, wt[k])
        if k == 0:
            pay[:, OWN_AT:PAY] = g
            pay0[:, OWN_AT:PAY] = g
            pay0[:, PAY + RANK:] = e
    q_part = (ADAPTER_SCALE * q_part).astype(BF)
    pay[:, Z_AT:OWN_AT] = q_part
    pay0[:, Z_AT:OWN_AT] = q_part
    pay0[:, PAY:PAY + RANK] = z_in[0]
    n = total.astype(BF)
    pay[:, :WIDE] = n
    pay0[:, :WIDE] = n


def gradient_kernel(sc, x, h, q, z, e, ga, gb, h_turned, z_turned):
    @pl.when(pl.program_id(0) == 0)
    def _():
        h_turned[...] = jnp.where(sc[1] == 0, x[...], h[...]).T
        z_turned[...] = z[...].T

    block = lax.broadcasted_iota(jnp.int32, (1, TOKENS), 1) // ROWS
    for i in range(STYLES_AT_ONCE):
        style = pl.program_id(0) * STYLES_AT_ONCE + i
        keep = jnp.zeros((1, TOKENS), F32)
        for n in range(BLOCKS):
            keep = jnp.where((block == n) & (sc[16 + n] == style), 1.0, keep)
        keep = keep.astype(BF)
        ga[i, 0] = dot(h_turned[...] * keep, q[...]).astype(BF)
        gb[i, 0] = (ADAPTER_SCALE * dot(z_turned[...] * keep, e[...])).astype(BF)


def slot_spec(slot, tick, columns):
    return pl.BlockSpec((1, ROWS, columns), lambda i, sc: (slot(tick, sc[1]), 0, 0))


def forward_tick(tick, scalars, payloads, rows, w, ab, g_buf, z_buf, h_buf):
    grid_spec = pltpu.PrefetchScalarGridSpec(
        num_scalar_prefetch=1,
        grid=(1,),
        in_specs=[IN_VMEM] * 7 + [ANYWHERE] * 3,
        out_specs=[IN_VMEM] + [slot_spec(forward_save, tick, columns) for columns in (WIDE, RANK, CHUNK)],
        scratch_shapes=[pltpu.VMEM((ROWS, WIDE), BF)],
    )
    return pl.pallas_call(
        functools.partial(forward_kernel, tick),
        grid_spec=grid_spec,
        out_shape=[shaped(ROWS, PAY)] + [shaped(*v.shape, dtype=v.dtype) for v in (g_buf, z_buf, h_buf)],
        input_output_aliases={8: 1, 9: 2, 10: 3},
        compiler_params=PARAMS,
        name="forward_stage",
    )(scalars, *payloads, rows, w, ab, g_buf, z_buf, h_buf)


def backward_tick(tick, scalars, payloads, rows, wt, ab, g_buf, z_buf, q_buf, zr_buf, e_buf):
    grid_spec = pltpu.PrefetchScalarGridSpec(
        num_scalar_prefetch=1,
        grid=(1,),
        in_specs=[IN_VMEM] * 7 + [slot_spec(backward_block, tick, columns) for columns in (WIDE, RANK)]
        + [ANYWHERE] * 3,
        out_specs=[IN_VMEM] * 2 + [slot_spec(backward_save, tick, columns) for columns in (RANK, RANK, CHUNK)],
    )
    return pl.pallas_call(
        functools.partial(backward_kernel, tick),
        grid_spec=grid_spec,
        out_shape=[shaped(ROWS, PAY_EXTRA), shaped(ROWS, PAY)]
        + [shaped(*v.shape, dtype=v.dtype) for v in (q_buf, zr_buf, e_buf)],
        input_output_aliases={10: 2, 11: 3, 12: 4},
        compiler_params=PARAMS,
        name="backward_stage",
    )(scalars, *payloads, rows, wt, ab, g_buf, z_buf, q_buf, zr_buf, e_buf)


def gradients(scalars, x_in, h_buf, q_buf, zr_buf, e_buf):
    flat = lambda v: v.reshape(-1, v.shape[-1])
    whole = lambda columns: pl.BlockSpec((TOKENS, columns), lambda i, sc: (0, 0))
    grid_spec = pltpu.PrefetchScalarGridSpec(
        num_scalar_prefetch=1,
        grid=(LAYERS // STYLES_AT_ONCE,),
        in_specs=[whole(CHUNK), whole(CHUNK), whole(RANK), whole(RANK), whole(CHUNK)],
        out_specs=[pl.BlockSpec((STYLES_AT_ONCE, 1, CHUNK, RANK), lambda i, sc: (i, 0, 0, 0)),
                   pl.BlockSpec((STYLES_AT_ONCE, 1, RANK, CHUNK), lambda i, sc: (i, 0, 0, 0))],
        scratch_shapes=[pltpu.VMEM((CHUNK, TOKENS), BF), pltpu.VMEM((RANK, TOKENS), BF)],
    )
    return pl.pallas_call(
        gradient_kernel,
        grid_spec=grid_spec,
        out_shape=[shaped(LAYERS, 1, CHUNK, RANK), shaped(LAYERS, 1, RANK, CHUNK)],
        compiler_params=PARAMS,
        name="style_gradients",
    )(scalars, x_in, flat(h_buf), flat(q_buf), flat(zr_buf), flat(e_buf))


def body(x_in, cotangent, weights, down_weight_store, lib_b, style_ids, slot_of):
    section = lax.axis_index("section")
    tp = lax.axis_index("tp")
    core, z_pos, y_pos = section % 2, tp // SIDE, tp % SIDE
    a = jnp.where(core == 0, y_pos, z_pos)
    b = jnp.where(core == 0, z_pos, y_pos)
    flat_ids = style_ids.reshape(-1)
    styles = jnp.arange(slot_of.shape[0], dtype=jnp.int32)
    slots = jnp.sum(jnp.where(flat_ids[:, None] == styles[None, :], slot_of[None, :], 0), axis=1)
    place = jnp.stack([core, section, a, b, 0, 0, 0, 0]).astype(jnp.int32)
    scalars = jnp.concatenate([place, slots, flat_ids])

    with jax.named_scope("adapters"):
        ab_out = pack_layers(down_weight_store, lib_b)
        raw, ab_out = lax.optimization_barrier((weights, ab_out))
        ab_in = lax.all_to_all(ab_out, "section", split_axis=0, concat_axis=0, tiled=True)
    with jax.named_scope("weight_blocks"):
        cut = copy_kernel("cut_weights", cut_weights_kernel, SIDE * SIDE, [shaped(SIDE, CHUNK, CHUNK)] * SIDE, ANYWHERE,
                          place, raw[0].reshape(SIDE * SIDE, CHUNK, CHUNK))
        cut = [piece.reshape(WIDE, CHUNK) for piece in cut]
        w_pieces = [cut[0]] + [send(cut[k], along_a(k)) for k in range(1, SIDE)]
    with jax.named_scope("blocks"):
        packed = copy_kernel("pack_blocks", pack_blocks_kernel, 2 + BLOCKS, shaped(PACKED, CHUNK),
                             ANYWHERE, scalars, x_in, cotangent, ab_in)
        below, above = send(packed, along_b(1)), send(packed, along_b(3))
        first = send(below[:PACKED // 2], along_b(1))
        second = send(above[PACKED // 2:], along_b(3))
        block_pieces = [packed, below, first, second, above]
    with jax.named_scope("weight_blocks"):
        w_pieces[0], _ = lax.optimization_barrier((w_pieces[0], packed))
        w_own = settle_weights(place, w_pieces)
        w_turned = transposed(w_own)
    with jax.named_scope("previous_weights"):
        w_prev = send(w_turned, onward(0))
    with jax.named_scope("blocks"):
        block_pieces[0], _ = lax.optimization_barrier((block_pieces[0], w_turned))
        x_rows, cot_rows, ab = settle_blocks(place, block_pieces)

    first_in = jnp.zeros((ROWS, PAY), BF)
    fwd_in = [first_in] * SIDE
    bwd_in = [jnp.zeros((ROWS, PAY_EXTRA), BF)] + [jnp.zeros((ROWS, PAY), BF)] * (SIDE - 1)
    buffer = lambda columns, dtype: jnp.zeros((BLOCKS + 1, ROWS, columns), dtype)
    g_buf, z_buf, h_buf = buffer(WIDE, F32), buffer(RANK, BF), buffer(CHUNK, BF)
    q_buf, zr_buf, e_buf = buffer(RANK, BF), buffer(RANK, BF), buffer(CHUNK, BF)
    for tick in range(2 * LAYERS + BLOCKS):
        if tick == 4:
            with jax.named_scope("previous_weights"):
                w_prev, fwd_in[0] = lax.optimization_barrier((w_prev, fwd_in[0]))
                w_prev = copy_kernel("settle_previous", settle_previous_kernel, SIDE, shaped(SIDE, CHUNK, WIDE),
                                     IN_VMEM, place, w_prev)
        if tick < LAYERS + BLOCKS:
            with jax.named_scope("forward"):
                pay, g_buf, z_buf, h_buf = forward_tick(
                    tick, place, fwd_in, x_rows, w_own, ab, g_buf, z_buf, h_buf)
                if tick < LAYERS + BLOCKS - 1:
                    fwd_in = [send(pay, onward(k)) for k in range(SIDE)]
        if tick >= LAYERS:
            with jax.named_scope("backward"):
                pay0, pay, q_buf, zr_buf, e_buf = backward_tick(
                    tick, place, bwd_in, cot_rows, w_prev, ab, g_buf, z_buf, q_buf, zr_buf, e_buf)
                if tick < 2 * LAYERS + BLOCKS - 1:
                    bwd_in = [send(pay0, backward(0))] + [send(pay, backward(k)) for k in range(1, SIDE)]
    with jax.named_scope("gradients"):
        grad_a, grad_b = gradients(scalars, x_in, h_buf, q_buf, zr_buf, e_buf)
    return grad_a, grad_b


def solution(mesh):
    in_specs = (
        P(None, "tp"),
        P(None, "tp"),
        P("section", None, "tp"),
        P("section", None, "tp", None),
        P("section", None, None, "tp"),
        P(),
        P(),
    )
    out_specs = (P(None, "section", "tp", None), P(None, "section", None, "tp"))
    return jax.shard_map(body, mesh=mesh, in_specs=in_specs, out_specs=out_specs, check_vma=False)
```

```python
import functools

import jax
import jax.numpy as jnp
from jax import lax
from jax.experimental import pallas as pl
from jax.experimental.pallas import tpu as pltpu
from jax.sharding import PartitionSpec as P

ADAPTER_SCALE = 0.25
SIDE = 4
LAYERS = 8
BLOCKS = 8
ROWS = 32
TOKENS = BLOCKS * ROWS
RANK = 128
CHUNK = 384
WIDE = SIDE * CHUNK
PARTS = CHUNK // RANK
PAIR = 2 * RANK
FIRST_BLOCKS = 4
LAST_FORWARD = LAYERS + BLOCKS - 1
LAST_BACKWARD = 2 * LAYERS + BLOCKS - 1
Z_AT = WIDE
OWN_AT = WIDE + RANK
PAY = OWN_AT + CHUNK
PAY_EXTRA = PAY + RANK + CHUNK
STYLES_AT_ONCE = 4
BF = jnp.bfloat16
F32 = jnp.float32


def along_a(k):
    return lambda x, c, z, y: (x, c, z, y + k) if c == 0 else (x, c, z + k, y)


def along_b(k):
    return lambda x, c, z, y: (x, c, z + k, y) if c == 0 else (x, c, z, y + k)


def onward(k):
    return lambda x, c, z, y: (x, 1, z, y + k) if c == 0 else (x + 1, 0, z + k, y)


def backward(k):
    return lambda x, c, z, y: (x, 0, z + k, y) if c == 1 else (x - 1, 1, z, y + k)


def send(value, target):
    pairs = []
    for sec in range(2 * SIDE):
        for tp in range(SIDE * SIDE):
            x, c, z, y = target(sec // 2, sec % 2, tp // SIDE, tp % SIDE)
            sec_to = (x % SIDE) * 2 + c
            tp_to = (z % SIDE) * SIDE + y % SIDE
            pairs.append((sec * SIDE * SIDE + tp, sec_to * SIDE * SIDE + tp_to))
    return lax.ppermute(value, ("section", "tp"), pairs)


IN_VMEM = pl.BlockSpec(memory_space=pltpu.VMEM)
IN_SMEM = pl.BlockSpec(memory_space=pltpu.SMEM)
ANYWHERE = pl.BlockSpec(memory_space=pl.ANY)
SMALL = pl.CostEstimate(flops=0, bytes_accessed=1024, transcendentals=0)
PARAMS = pltpu.CompilerParams(vmem_limit_bytes=16 << 20)


def shaped(*shape, dtype=BF):
    return jax.ShapeDtypeStruct(shape, dtype)


def chunk_at(index):
    return pl.ds(pl.multiple_of(index * CHUNK, CHUNK), CHUNK)


def dot(left, right):
    return jnp.dot(left, right, preferred_element_type=F32)


def dot_nt(left, right):
    return lax.dot_general(left, right, (((1,), (1,)), ((), ())), preferred_element_type=F32)


def dot_tn(left, right):
    return lax.dot_general(left, right, (((0,), (0,)), ((), ())), preferred_element_type=F32)


def parts(value):
    return [value[:, part * RANK:(part + 1) * RANK] for part in range(PARTS)]


def gelu_both(y):
    scale = 0.7978845608028654
    square = y * y
    t = jnp.tanh(scale * y * (1.0 + 0.044715 * square))
    half = 0.5 * (1.0 + t)
    slope = half + 0.5 * y * (1.0 - t * t) * scale * (1.0 + 3.0 * 0.044715 * square)
    return y * half, slope


def run_copies(moves, sems):
    copies = [pltpu.make_async_copy(source, target, sems.at[i]) for i, (source, target) in enumerate(moves)]
    for copy in copies:
        copy.start()
    for copy in copies:
        copy.wait()


def copy_kernel(name, kernel, count, out_shape, out_spec, scalars, *operands):
    many = isinstance(out_shape, list)
    return pl.pallas_call(
        kernel,
        in_specs=[IN_SMEM] + [ANYWHERE] * len(operands),
        out_specs=[out_spec] * len(out_shape) if many else out_spec,
        out_shape=out_shape,
        scratch_shapes=[pltpu.SemaphoreType.DMA((count,))],
        compiler_params=PARAMS,
        cost_estimate=SMALL,
        name=name,
    )(scalars, *operands)


def pack_layers_kernel(a, b, out):
    for layer in range(LAYERS):
        for part in range(PARTS):
            out[layer, :RANK, part * RANK:(part + 1) * RANK] = a[0, layer, part * RANK:(part + 1) * RANK]
        out[layer, RANK:] = b[0, (layer - 1) % LAYERS]


def pack_layers(a, b):
    return pl.pallas_call(
        pack_layers_kernel,
        in_specs=[IN_VMEM] * 2,
        out_specs=IN_VMEM,
        out_shape=shaped(LAYERS, PAIR, CHUNK),
        compiler_params=PARAMS,
        name="pack_layers",
    )(a, b)


def cut_weights_kernel(sc, w, o0, o1, o2, o3, sems):
    core, a = sc[0], sc[2]
    moves = []
    for k, out in enumerate((o0, o1, o2, o3)):
        to = lax.rem(a + k, SIDE)
        for j in range(SIDE):
            source = jnp.where(core == 0, j * SIDE + to, to * SIDE + j)
            moves.append((w.at[source], out.at[j]))
    run_copies(moves, sems)


def pack_blocks_kernel(sc, x, ab, first, second, sems):
    moves = [(x, first.at[pl.ds(0, TOKENS)])]
    for n in range(BLOCKS):
        out, start = (first, TOKENS + n * PAIR) if n < FIRST_BLOCKS else (second, (n - FIRST_BLOCKS) * PAIR)
        moves.append((ab.at[sc[8 + n]], out.at[pl.ds(start, PAIR)]))
    run_copies(moves, sems)


def settle_weights_kernel(sc, own, w1, w2, w3, out, sems):
    copies = [pltpu.make_async_copy(w, out.at[k + 1], sems.at[k]) for k, w in enumerate((w1, w2, w3))]
    for copy in copies:
        copy.start()
    out[0] = own[...]
    for copy in copies:
        copy.wait()


def settle_weights(scalars, pieces):
    return pl.pallas_call(
        settle_weights_kernel,
        in_specs=[IN_SMEM, IN_VMEM] + [ANYWHERE] * (SIDE - 1),
        out_specs=IN_VMEM,
        out_shape=shaped(SIDE, WIDE, CHUNK),
        scratch_shapes=[pltpu.SemaphoreType.DMA((SIDE - 1,))],
        compiler_params=PARAMS,
        cost_estimate=SMALL,
        name="settle_weights",
    )(scalars, *pieces)


def settle_blocks_kernel(sc, f0, s0, f1, s1, f2, s2, f3, s3, x, ab, sems):
    early, late = pl.ds(0, FIRST_BLOCKS * PAIR), pl.ds(FIRST_BLOCKS * PAIR, (BLOCKS - FIRST_BLOCKS) * PAIR)
    head, tail = pl.ds(0, TOKENS), pl.ds(TOKENS, FIRST_BLOCKS * PAIR)
    copies = []
    for k, (first, second) in ((1, (f1, s1)), (2, (f2, s2)), (3, (f3, s3))):
        for i, (source, target) in enumerate((
                (first.at[head], x.at[k]), (first.at[tail], ab.at[k, early]), (second, ab.at[k, late]))):
            copies.append(pltpu.make_async_copy(source, target, sems.at[k - 1, i]))
    for copy in copies:
        copy.start()
    x[0] = f0[head]
    ab[0, early] = f0[tail]
    ab[0, late] = s0[...]
    for copy in copies:
        copy.wait()


def settle_blocks(scalars, pieces):
    return pl.pallas_call(
        settle_blocks_kernel,
        in_specs=[IN_SMEM, IN_VMEM, IN_VMEM] + [ANYWHERE] * 6,
        out_specs=[IN_VMEM] * 2,
        out_shape=[shaped(SIDE, TOKENS, CHUNK), shaped(SIDE, BLOCKS * PAIR, CHUNK)],
        scratch_shapes=[pltpu.SemaphoreType.DMA((SIDE - 1, 3))],
        compiler_params=PARAMS,
        cost_estimate=SMALL,
        name="settle_blocks",
    )(scalars, *pieces)


def settle_previous_kernel(sc, first, rest, out, sems):
    run_copies([(first.at[0], out.at[0])] + [(rest.at[k - 1], out.at[k]) for k in range(1, SIDE)], sems)


def transpose_kernel(w, out):
    out[0] = w[0].T


def transposed(w, begin, end):
    return pl.pallas_call(
        transpose_kernel,
        grid=(end - begin,),
        in_specs=[pl.BlockSpec((1, WIDE, CHUNK), lambda i: (i + begin, 0, 0))],
        out_specs=pl.BlockSpec((1, CHUNK, WIDE), lambda i: (i, 0, 0)),
        out_shape=shaped(end - begin, CHUNK, WIDE),
        compiler_params=PARAMS,
        cost_estimate=SMALL,
        name="transpose_weights",
    )(w)


def within(index):
    return jnp.clip(index, 0, BLOCKS - 1)


def slot_or_spare(index):
    return jnp.where((index >= 0) & (index < BLOCKS), index, BLOCKS)


def forward_block(tick, section):
    return within(tick - jnp.where((section == 0) & (tick >= LAYERS), LAYERS, section))


def boundary(section):
    return jnp.where(section == 0, LAYERS, section)


def forward_save(tick, section):
    return slot_or_spare(tick - boundary(section))


def backward_block(tick, section):
    return within(tick - 2 * LAYERS + boundary(section))


def backward_save(tick, section):
    return slot_or_spare(tick - 2 * LAYERS + section)


def forward_kernel(tick, sc, p0, p1, p2, p3, rows, cot, w, ab, _g, _z, _h, pay, g_out, z_out, h_out, h_all):
    section, a, b = sc[1], sc[2], sc[3]
    block = forward_block(tick, section)
    own_rows = pl.ds(pl.multiple_of(block * ROWS, ROWS), ROWS)
    down = pl.ds(pl.multiple_of(block * PAIR, PAIR), RANK)
    up = pl.ds(pl.multiple_of(block * PAIR + RANK, RANK), RANK)
    z = sum(p[:, Z_AT:OWN_AT].astype(F32) for p in (p0, p1, p2, p3)).astype(BF)
    z_out[0] = z
    z_part = jnp.zeros((ROWS, RANK), F32)
    for k, p in enumerate((p0, p1, p2, p3)):
        here = chunk_at(lax.rem(b - k + SIDE, SIDE))
        y = sum(q[:, here].astype(F32) for q in (p0, p1, p2, p3))
        value, slope = gelu_both(y + ADAPTER_SCALE * dot(z, ab[k, up]))
        h = (p[:, OWN_AT:PAY].astype(F32) + value).astype(BF)
        if tick < LAYERS:
            h = jnp.where(section == 0, rows[k, own_rows], h)
        h_all[:, here] = h
        g_out[0, :, here] = slope
        if tick < LAST_FORWARD:
            for piece, weight in zip(parts(h), parts(ab[k, down])):
                z_part = z_part + dot(piece, weight)
        if k == 0:
            h_out[0] = h
            pay[:, OWN_AT:PAY] = jnp.where(section == LAYERS - 1, cot[own_rows], h)
    pay[:, Z_AT:OWN_AT] = z_part.astype(BF)
    if tick == LAST_FORWARD:
        return
    h = h_all[...]
    for k in range(SIDE):
        pay[:, chunk_at(lax.rem(a - k + SIDE, SIDE))] = dot(h, w[k]).astype(BF)


def backward_kernel(tick, sc, q0, q1, q2, q3, p0, p1, p2, p3, wt, ab, slope, z_in,
                    _q, _z, _e, pay0, pay, q_out, z_out, e_out):
    section, b = sc[1], sc[3]
    block = backward_block(tick, section)
    q = sum(p[:, Z_AT:OWN_AT].astype(F32) for p in (q0, q1, q2, q3)).astype(BF)
    q_out[0] = q
    z_out[0] = q0[:, PAY:PAY + RANK]
    e_out[0] = q0[:, PAY + RANK:]
    if tick == LAST_BACKWARD:
        return
    q_part = jnp.zeros((ROWS, RANK), F32)
    total = jnp.zeros((ROWS, WIDE), F32)
    down = pl.ds(pl.multiple_of(block * PAIR, PAIR), RANK)
    up = pl.ds(pl.multiple_of(block * PAIR + RANK, RANK), RANK)
    for k, (p, cot) in enumerate(((q0, p0), (q1, p1), (q2, p2), (q3, p3))):
        here = chunk_at(lax.rem(b - k + SIDE, SIDE))
        n = sum(r[:, here].astype(F32) for r in (q0, q1, q2, q3))
        back = jnp.concatenate([dot_nt(q, weight) for weight in parts(ab[k, down])], axis=1)
        g = (p[:, OWN_AT:PAY].astype(F32) + n + back).astype(BF)
        if tick <= LAST_FORWARD:
            g = jnp.where(section == 0, cot[:, OWN_AT:PAY], g)
        e = (slope[0, :, here] * g.astype(F32)).astype(BF)
        q_part = q_part + dot_nt(e, ab[k, up])
        total = total + dot(e, wt[k])
        if k == 0:
            pay[:, OWN_AT:PAY] = g
            pay0[:, OWN_AT:PAY] = g
            pay0[:, PAY + RANK:] = e
    q_part = (ADAPTER_SCALE * q_part).astype(BF)
    pay[:, Z_AT:OWN_AT] = q_part
    pay0[:, Z_AT:OWN_AT] = q_part
    pay0[:, PAY:PAY + RANK] = z_in[0]
    n = total.astype(BF)
    pay[:, :WIDE] = n
    pay0[:, :WIDE] = n


def gradient_kernel(sc, x, h, q, z, e, ga, gb, h_turned, z_turned):
    @pl.when(pl.program_id(0) == 0)
    def _():
        h_turned[...] = jnp.where(sc[1] == 0, x[...], h[...]).T
        z_turned[...] = z[...].T

    block = lax.broadcasted_iota(jnp.int32, (1, TOKENS), 1) // ROWS
    for i in range(STYLES_AT_ONCE):
        style = pl.program_id(0) * STYLES_AT_ONCE + i
        keep = jnp.zeros((1, TOKENS), F32)
        for n in range(BLOCKS):
            keep = jnp.where((block == n) & (sc[16 + n] == style), 1.0, keep)
        keep = keep.astype(BF)
        ga[i, 0] = dot(h_turned[...] * keep, q[...]).astype(BF)
        gb[i, 0] = (ADAPTER_SCALE * dot(z_turned[...] * keep, e[...])).astype(BF)


def slot_spec(slot, tick, columns):
    return pl.BlockSpec((1, ROWS, columns), lambda i, sc: (slot(tick, sc[1]), 0, 0))


def forward_tick(tick, scalars, payloads, rows, cot, w, ab, g_buf, z_buf, h_buf):
    grid_spec = pltpu.PrefetchScalarGridSpec(
        num_scalar_prefetch=1,
        grid=(1,),
        in_specs=[IN_VMEM] * 8 + [ANYWHERE] * 3,
        out_specs=[IN_VMEM] + [slot_spec(forward_save, tick, columns) for columns in (WIDE, RANK, CHUNK)],
        scratch_shapes=[pltpu.VMEM((ROWS, WIDE), BF)],
    )
    return pl.pallas_call(
        functools.partial(forward_kernel, tick),
        grid_spec=grid_spec,
        out_shape=[shaped(ROWS, PAY)] + [shaped(*v.shape, dtype=v.dtype) for v in (g_buf, z_buf, h_buf)],
        input_output_aliases={9: 1, 10: 2, 11: 3},
        compiler_params=PARAMS,
        name="forward_stage",
    )(scalars, *payloads, rows, cot, w, ab, g_buf, z_buf, h_buf)


def backward_tick(tick, scalars, payloads, last_in, wt, ab, g_buf, z_buf, q_buf, zr_buf, e_buf):
    grid_spec = pltpu.PrefetchScalarGridSpec(
        num_scalar_prefetch=1,
        grid=(1,),
        in_specs=[IN_VMEM] * 10 + [slot_spec(backward_block, tick, columns) for columns in (WIDE, RANK)]
        + [ANYWHERE] * 3,
        out_specs=[IN_VMEM] * 2 + [slot_spec(backward_save, tick, columns) for columns in (RANK, RANK, CHUNK)],
    )
    return pl.pallas_call(
        functools.partial(backward_kernel, tick),
        grid_spec=grid_spec,
        out_shape=[shaped(ROWS, PAY_EXTRA), shaped(ROWS, PAY)]
        + [shaped(*v.shape, dtype=v.dtype) for v in (q_buf, zr_buf, e_buf)],
        input_output_aliases={13: 2, 14: 3, 15: 4},
        compiler_params=PARAMS,
        name="backward_stage",
    )(scalars, *payloads, *last_in, wt, ab, g_buf, z_buf, q_buf, zr_buf, e_buf)


def gradients(scalars, x_in, h_buf, q_buf, zr_buf, e_buf):
    flat = lambda v: v.reshape(-1, v.shape[-1])
    whole = lambda columns: pl.BlockSpec((TOKENS, columns), lambda i, sc: (0, 0))
    grid_spec = pltpu.PrefetchScalarGridSpec(
        num_scalar_prefetch=1,
        grid=(LAYERS // STYLES_AT_ONCE,),
        in_specs=[whole(CHUNK), whole(CHUNK), whole(RANK), whole(RANK), whole(CHUNK)],
        out_specs=[pl.BlockSpec((STYLES_AT_ONCE, 1, CHUNK, RANK), lambda i, sc: (i, 0, 0, 0)),
                   pl.BlockSpec((STYLES_AT_ONCE, 1, RANK, CHUNK), lambda i, sc: (i, 0, 0, 0))],
        scratch_shapes=[pltpu.VMEM((CHUNK, TOKENS), BF), pltpu.VMEM((RANK, TOKENS), BF)],
    )
    return pl.pallas_call(
        gradient_kernel,
        grid_spec=grid_spec,
        out_shape=[shaped(LAYERS, 1, CHUNK, RANK), shaped(LAYERS, 1, RANK, CHUNK)],
        compiler_params=PARAMS,
        name="style_gradients",
    )(scalars, x_in, flat(h_buf), flat(q_buf), flat(zr_buf), flat(e_buf))


def body(x_in, cotangent, weights, down_weight_store, lib_b, style_ids, slot_of):
    section = lax.axis_index("section")
    tp = lax.axis_index("tp")
    core, z_pos, y_pos = section % 2, tp // SIDE, tp % SIDE
    a = jnp.where(core == 0, y_pos, z_pos)
    b = jnp.where(core == 0, z_pos, y_pos)
    flat_ids = style_ids.reshape(-1)
    styles = jnp.arange(slot_of.shape[0], dtype=jnp.int32)
    slots = jnp.sum(jnp.where(flat_ids[:, None] == styles[None, :], slot_of[None, :], 0), axis=1)
    place = jnp.stack([core, section, a, b, 0, 0, 0, 0]).astype(jnp.int32)
    scalars = jnp.concatenate([place, slots, flat_ids])

    with jax.named_scope("adapters"):
        ab_out = pack_layers(down_weight_store, lib_b)
        raw, ab_out = lax.optimization_barrier((weights, ab_out))
        ab_in = lax.all_to_all(ab_out, "section", split_axis=0, concat_axis=0, tiled=True)
    with jax.named_scope("weight_blocks"):
        cut = copy_kernel("cut_weights", cut_weights_kernel, SIDE * SIDE, [shaped(SIDE, CHUNK, CHUNK)] * SIDE, ANYWHERE,
                          place, raw[0].reshape(SIDE * SIDE, CHUNK, CHUNK))
        cut = [piece.reshape(WIDE, CHUNK) for piece in cut]
        w_pieces = [cut[0]] + [send(cut[k], along_a(k)) for k in range(1, SIDE)]
        w_prev_first = send(transposed(cut[0][None], 0, 1), onward(0))
    with jax.named_scope("blocks"):
        first, second = copy_kernel(
            "pack_blocks", pack_blocks_kernel, 1 + BLOCKS,
            [shaped(TOKENS + FIRST_BLOCKS * PAIR, CHUNK), shaped((BLOCKS - FIRST_BLOCKS) * PAIR, CHUNK)], ANYWHERE,
            scalars, x_in, ab_in)
        first_below, second_above = send(first, along_b(1)), send(second, along_b(3))
        second_below, first_above = send(second, along_b(1)), send(first, along_b(3))
        first_far, second_far = send(first_below, along_b(1)), send(second_above, along_b(3))
        block_pieces = [first, second, first_below, second_below, first_far, second_far, first_above, second_above]
    with jax.named_scope("weight_blocks"):
        w_pieces[0], w_prev_first, _ = lax.optimization_barrier((w_pieces[0], w_prev_first, first))
        w_own = settle_weights(place, w_pieces)
        w_turned = transposed(w_own, 1, SIDE)
    with jax.named_scope("previous_weights"):
        w_prev = send(w_turned, onward(0))
    with jax.named_scope("blocks"):
        block_pieces[0], _ = lax.optimization_barrier((block_pieces[0], w_turned))
        x_rows, ab = settle_blocks(place, block_pieces)

    first_in = jnp.zeros((ROWS, PAY), BF)
    fwd_in = [first_in] * SIDE
    bwd_in = [jnp.zeros((ROWS, PAY_EXTRA), BF)] + [jnp.zeros((ROWS, PAY), BF)] * (SIDE - 1)
    buffer = lambda columns, dtype: jnp.zeros((BLOCKS + 1, ROWS, columns), dtype)
    g_buf, z_buf, h_buf = buffer(WIDE, F32), buffer(RANK, BF), buffer(CHUNK, BF)
    q_buf, zr_buf, e_buf = buffer(RANK, BF), buffer(RANK, BF), buffer(CHUNK, BF)
    for tick in range(2 * LAYERS + BLOCKS):
        if tick == 4:
            with jax.named_scope("previous_weights"):
                w_prev, fwd_in[0] = lax.optimization_barrier((w_prev, fwd_in[0]))
                w_prev = copy_kernel("settle_previous", settle_previous_kernel, SIDE, shaped(SIDE, CHUNK, WIDE),
                                     IN_VMEM, place, w_prev_first, w_prev)
        if tick < LAYERS + BLOCKS:
            with jax.named_scope("forward"):
                last_in = fwd_in
                pay, g_buf, z_buf, h_buf = forward_tick(
                    tick, place, fwd_in, x_rows, cotangent, w_own, ab, g_buf, z_buf, h_buf)
                if tick < LAYERS + BLOCKS - 1:
                    fwd_in = [send(pay, onward(k)) for k in range(SIDE)]
        if tick >= LAYERS:
            with jax.named_scope("backward"):
                pay0, pay, q_buf, zr_buf, e_buf = backward_tick(
                    tick, place, bwd_in, last_in, w_prev, ab, g_buf, z_buf, q_buf, zr_buf, e_buf)
                if tick < 2 * LAYERS + BLOCKS - 1:
                    bwd_in = [send(pay0, backward(0))] + [send(pay, backward(k)) for k in range(1, SIDE)]
    with jax.named_scope("gradients"):
        grad_a, grad_b = gradients(scalars, x_in, h_buf, q_buf, zr_buf, e_buf)
    return grad_a, grad_b


def solution(mesh):
    in_specs = (
        P(None, "tp"),
        P(None, "tp"),
        P("section", None, "tp"),
        P("section", None, "tp", None),
        P("section", None, None, "tp"),
        P(),
        P(),
    )
    out_specs = (P(None, "section", "tp", None), P(None, "section", None, "tp"))
    return jax.shard_map(body, mesh=mesh, in_specs=in_specs, out_specs=out_specs, check_vma=False)
```

```python
import functools

import jax
import jax.numpy as jnp
from jax import lax
from jax.experimental import pallas as pl
from jax.experimental.pallas import tpu as pltpu
from jax.sharding import PartitionSpec as P

ADAPTER_SCALE = 0.25
SIDE = 4
LAYERS = 8
BLOCKS = 8
ROWS = 32
TOKENS = BLOCKS * ROWS
RANK = 128
CHUNK = 384
WIDE = SIDE * CHUNK
PARTS = CHUNK // RANK
PAIR = 2 * RANK
FIRST_BLOCKS = 4
LAST_FORWARD = LAYERS + BLOCKS - 1
LAST_BACKWARD = 2 * LAYERS + BLOCKS - 1
Z_AT = WIDE
OWN_AT = WIDE + RANK
PAY = OWN_AT + CHUNK
PAY_EXTRA = PAY + RANK + CHUNK
STYLES_AT_ONCE = 4
BF = jnp.bfloat16
F32 = jnp.float32


def along_a(k):
    return lambda x, c, z, y: (x, c, z, y + k) if c == 0 else (x, c, z + k, y)


def along_b(k):
    return lambda x, c, z, y: (x, c, z + k, y) if c == 0 else (x, c, z, y + k)


def onward(k):
    return lambda x, c, z, y: (x, 1, z, y + k) if c == 0 else (x + 1, 0, z + k, y)


def backward(k):
    return lambda x, c, z, y: (x, 0, z + k, y) if c == 1 else (x - 1, 1, z, y + k)


def send(value, target):
    pairs = []
    for sec in range(2 * SIDE):
        for tp in range(SIDE * SIDE):
            x, c, z, y = target(sec // 2, sec % 2, tp // SIDE, tp % SIDE)
            sec_to = (x % SIDE) * 2 + c
            tp_to = (z % SIDE) * SIDE + y % SIDE
            pairs.append((sec * SIDE * SIDE + tp, sec_to * SIDE * SIDE + tp_to))
    return lax.ppermute(value, ("section", "tp"), pairs)


IN_VMEM = pl.BlockSpec(memory_space=pltpu.VMEM)
IN_SMEM = pl.BlockSpec(memory_space=pltpu.SMEM)
ANYWHERE = pl.BlockSpec(memory_space=pl.ANY)
SMALL = pl.CostEstimate(flops=0, bytes_accessed=1024, transcendentals=0)
PARAMS = pltpu.CompilerParams(vmem_limit_bytes=16 << 20)


def shaped(*shape, dtype=BF):
    return jax.ShapeDtypeStruct(shape, dtype)


def chunk_at(index):
    return pl.ds(pl.multiple_of(index * CHUNK, CHUNK), CHUNK)


def dot(left, right):
    return jnp.dot(left, right, preferred_element_type=F32)


def dot_nt(left, right):
    return lax.dot_general(left, right, (((1,), (1,)), ((), ())), preferred_element_type=F32)


def dot_tn(left, right):
    return lax.dot_general(left, right, (((0,), (0,)), ((), ())), preferred_element_type=F32)


def parts(value):
    return [value[:, part * RANK:(part + 1) * RANK] for part in range(PARTS)]


def gelu_both(y):
    scale = 0.7978845608028654
    square = y * y
    t = jnp.tanh(scale * y * (1.0 + 0.044715 * square))
    half = 0.5 * (1.0 + t)
    slope = half + 0.5 * y * (1.0 - t * t) * scale * (1.0 + 3.0 * 0.044715 * square)
    return y * half, slope


def run_copies(moves, sems):
    copies = [pltpu.make_async_copy(source, target, sems.at[i]) for i, (source, target) in enumerate(moves)]
    for copy in copies:
        copy.start()
    for copy in copies:
        copy.wait()


def copy_kernel(name, kernel, count, out_shape, out_spec, scalars, *operands):
    many = isinstance(out_shape, list)
    return pl.pallas_call(
        kernel,
        in_specs=[IN_SMEM] + [ANYWHERE] * len(operands),
        out_specs=[out_spec] * len(out_shape) if many else out_spec,
        out_shape=out_shape,
        scratch_shapes=[pltpu.SemaphoreType.DMA((count,))],
        compiler_params=PARAMS,
        cost_estimate=SMALL,
        name=name,
    )(scalars, *operands)


def pack_layers_kernel(a, b, out):
    for layer in range(LAYERS):
        for part in range(PARTS):
            out[layer, :RANK, part * RANK:(part + 1) * RANK] = a[0, layer, part * RANK:(part + 1) * RANK]
        out[layer, RANK:] = b[0, (layer - 1) % LAYERS]


def pack_layers(a, b):
    return pl.pallas_call(
        pack_layers_kernel,
        in_specs=[IN_VMEM] * 2,
        out_specs=IN_VMEM,
        out_shape=shaped(LAYERS, PAIR, CHUNK),
        compiler_params=PARAMS,
        name="pack_layers",
    )(a, b)


def cut_weights_kernel(sc, w, o0, o1, o2, o3, sems):
    core, a = sc[0], sc[2]
    moves = []
    for k, out in enumerate((o0, o1, o2, o3)):
        to = lax.rem(a + k, SIDE)
        for j in range(SIDE):
            source = jnp.where(core == 0, j * SIDE + to, to * SIDE + j)
            moves.append((w.at[source], out.at[j]))
    run_copies(moves, sems)


def pack_blocks_kernel(sc, x, ab, first, second, sems):
    moves = [(x, first.at[pl.ds(0, TOKENS)])]
    for n in range(BLOCKS):
        out, start = (first, TOKENS + n * PAIR) if n < FIRST_BLOCKS else (second, (n - FIRST_BLOCKS) * PAIR)
        moves.append((ab.at[sc[8 + n]], out.at[pl.ds(start, PAIR)]))
    run_copies(moves, sems)


def settle_weights_kernel(sc, own, w1, w2, w3, out, sems):
    copies = [pltpu.make_async_copy(w, out.at[k + 1], sems.at[k]) for k, w in enumerate((w1, w2, w3))]
    for copy in copies:
        copy.start()
    out[0] = own[...]
    for copy in copies:
        copy.wait()


def settle_weights(scalars, pieces):
    return pl.pallas_call(
        settle_weights_kernel,
        in_specs=[IN_SMEM, IN_VMEM] + [ANYWHERE] * (SIDE - 1),
        out_specs=IN_VMEM,
        out_shape=shaped(SIDE, WIDE, CHUNK),
        scratch_shapes=[pltpu.SemaphoreType.DMA((SIDE - 1,))],
        compiler_params=PARAMS,
        cost_estimate=SMALL,
        name="settle_weights",
    )(scalars, *pieces)


def settle_blocks_kernel(sc, f0, s0, f1, s1, f2, s2, f3, s3, x, ab, sems):
    early, late = pl.ds(0, FIRST_BLOCKS * PAIR), pl.ds(FIRST_BLOCKS * PAIR, (BLOCKS - FIRST_BLOCKS) * PAIR)
    head, tail = pl.ds(0, TOKENS), pl.ds(TOKENS, FIRST_BLOCKS * PAIR)
    copies = []
    for k, (first, second) in ((1, (f1, s1)), (2, (f2, s2)), (3, (f3, s3))):
        for i, (source, target) in enumerate((
                (first.at[head], x.at[k]), (first.at[tail], ab.at[k, early]), (second, ab.at[k, late]))):
            copies.append(pltpu.make_async_copy(source, target, sems.at[k - 1, i]))
    for copy in copies:
        copy.start()
    x[0] = f0[head]
    ab[0, early] = f0[tail]
    ab[0, late] = s0[...]
    for copy in copies:
        copy.wait()


def settle_blocks(scalars, pieces):
    return pl.pallas_call(
        settle_blocks_kernel,
        in_specs=[IN_SMEM, IN_VMEM, IN_VMEM] + [ANYWHERE] * 6,
        out_specs=[IN_VMEM] * 2,
        out_shape=[shaped(SIDE, TOKENS, CHUNK), shaped(SIDE, BLOCKS * PAIR, CHUNK)],
        scratch_shapes=[pltpu.SemaphoreType.DMA((SIDE - 1, 3))],
        compiler_params=PARAMS,
        cost_estimate=SMALL,
        name="settle_blocks",
    )(scalars, *pieces)


def settle_previous_kernel(sc, first, rest, out, sems):
    run_copies([(first.at[0], out.at[0])] + [(rest.at[k - 1], out.at[k]) for k in range(1, SIDE)], sems)


def transpose_kernel(w, out):
    out[0] = w[0].T


def transposed(w, begin, end):
    return pl.pallas_call(
        transpose_kernel,
        grid=(end - begin,),
        in_specs=[pl.BlockSpec((1, WIDE, CHUNK), lambda i: (i + begin, 0, 0))],
        out_specs=pl.BlockSpec((1, CHUNK, WIDE), lambda i: (i, 0, 0)),
        out_shape=shaped(end - begin, CHUNK, WIDE),
        compiler_params=PARAMS,
        cost_estimate=SMALL,
        name="transpose_weights",
    )(w)


def within(index):
    return jnp.clip(index, 0, BLOCKS - 1)


def slot_or_spare(index):
    return jnp.where((index >= 0) & (index < BLOCKS), index, BLOCKS)


def forward_block(tick, section):
    return within(tick - jnp.where((section == 0) & (tick >= LAYERS), LAYERS, section))


def boundary(section):
    return jnp.where(section == 0, LAYERS, section)


def forward_save(tick, section):
    return slot_or_spare(tick - boundary(section))


def backward_block(tick, section):
    return within(tick - 2 * LAYERS + boundary(section))


def backward_save(tick, section):
    return slot_or_spare(tick - 2 * LAYERS + section)


def forward_kernel(tick, sc, p0, p1, p2, p3, rows, cot, w, ab, _g, _z, _h, pay, g_out, z_out, h_out, h_all):
    section, a, b = sc[1], sc[2], sc[3]
    block = forward_block(tick, section)
    own_rows = pl.ds(pl.multiple_of(block * ROWS, ROWS), ROWS)
    down = pl.ds(pl.multiple_of(block * PAIR, PAIR), RANK)
    up = pl.ds(pl.multiple_of(block * PAIR + RANK, RANK), RANK)
    z = sum(p[:, Z_AT:OWN_AT].astype(F32) for p in (p0, p1, p2, p3)).astype(BF)
    z_out[0] = z
    z_part = jnp.zeros((ROWS, RANK), F32)
    for k, p in enumerate((p0, p1, p2, p3)):
        here = chunk_at(lax.rem(b - k + SIDE, SIDE))
        y = sum(q[:, here].astype(F32) for q in (p0, p1, p2, p3))
        value, slope = gelu_both(y + ADAPTER_SCALE * dot(z, ab[k, up]))
        h = (p[:, OWN_AT:PAY].astype(F32) + value).astype(BF)
        if tick < LAYERS:
            h = jnp.where(section == 0, rows[k, own_rows], h)
        h_all[:, here] = h
        g_out[0, :, here] = slope
        if tick < LAST_FORWARD:
            for piece, weight in zip(parts(h), parts(ab[k, down])):
                z_part = z_part + dot(piece, weight)
        if k == 0:
            h_out[0] = h
            pay[:, OWN_AT:PAY] = jnp.where(section == LAYERS - 1, cot[own_rows], h)
    pay[:, Z_AT:OWN_AT] = z_part.astype(BF)
    if tick == LAST_FORWARD:
        return
    h = h_all[...]
    for k in range(SIDE):
        pay[:, chunk_at(lax.rem(a - k + SIDE, SIDE))] = dot(h, w[k]).astype(BF)


def backward_kernel(tick, sc, q0, q1, q2, q3, p0, p1, p2, p3, wt, ab, slope, z_in,
                    _q, _z, _e, pay0, pay, q_out, z_out, e_out):
    section, b = sc[1], sc[3]
    block = backward_block(tick, section)
    q = sum(p[:, Z_AT:OWN_AT].astype(F32) for p in (q0, q1, q2, q3)).astype(BF)
    q_out[0] = q
    z_out[0] = q0[:, PAY:PAY + RANK]
    e_out[0] = q0[:, PAY + RANK:]
    if tick == LAST_BACKWARD:
        return
    q_part = jnp.zeros((ROWS, RANK), F32)
    total = jnp.zeros((ROWS, WIDE), F32)
    down = pl.ds(pl.multiple_of(block * PAIR, PAIR), RANK)
    up = pl.ds(pl.multiple_of(block * PAIR + RANK, RANK), RANK)
    for k, (p, cot) in enumerate(((q0, p0), (q1, p1), (q2, p2), (q3, p3))):
        here = chunk_at(lax.rem(b - k + SIDE, SIDE))
        n = sum(r[:, here].astype(F32) for r in (q0, q1, q2, q3))
        back = jnp.concatenate([dot_nt(q, weight) for weight in parts(ab[k, down])], axis=1)
        g = (p[:, OWN_AT:PAY].astype(F32) + n + back).astype(BF)
        if tick <= LAST_FORWARD:
            g = jnp.where(section == 0, cot[:, OWN_AT:PAY], g)
        e = (slope[0, :, here] * g.astype(F32)).astype(BF)
        q_part = q_part + dot_nt(e, ab[k, up])
        total = total + dot(e, wt[k])
        if k == 0:
            pay[:, OWN_AT:PAY] = g
            pay0[:, OWN_AT:PAY] = g
            pay0[:, PAY + RANK:] = e
    q_part = (ADAPTER_SCALE * q_part).astype(BF)
    pay[:, Z_AT:OWN_AT] = q_part
    pay0[:, Z_AT:OWN_AT] = q_part
    pay0[:, PAY:PAY + RANK] = z_in[0]
    n = total.astype(BF)
    pay[:, :WIDE] = n
    pay0[:, :WIDE] = n


def gradient_kernel(sc, x, h, q, z, e, ga, gb, h_turned, z_turned):
    @pl.when(pl.program_id(0) == 0)
    def _():
        h_turned[...] = jnp.where(sc[1] == 0, x[...], h[...]).T
        z_turned[...] = z[...].T

    block = lax.broadcasted_iota(jnp.int32, (1, TOKENS), 1) // ROWS
    for i in range(STYLES_AT_ONCE):
        style = pl.program_id(0) * STYLES_AT_ONCE + i
        keep = jnp.zeros((1, TOKENS), F32)
        for n in range(BLOCKS):
            keep = jnp.where((block == n) & (sc[16 + n] == style), 1.0, keep)
        keep = keep.astype(BF)
        ga[i, 0] = dot(h_turned[...] * keep, q[...]).astype(BF)
        gb[i, 0] = (ADAPTER_SCALE * dot(z_turned[...] * keep, e[...])).astype(BF)


def slot_spec(slot, tick, columns):
    return pl.BlockSpec((1, ROWS, columns), lambda i, sc: (slot(tick, sc[1]), 0, 0))


def forward_tick(tick, scalars, payloads, rows, cot, w, ab, g_buf, z_buf, h_buf):
    grid_spec = pltpu.PrefetchScalarGridSpec(
        num_scalar_prefetch=1,
        grid=(1,),
        in_specs=[IN_VMEM] * 8 + [ANYWHERE] * 3,
        out_specs=[IN_VMEM] + [slot_spec(forward_save, tick, columns) for columns in (WIDE, RANK, CHUNK)],
        scratch_shapes=[pltpu.VMEM((ROWS, WIDE), BF)],
    )
    return pl.pallas_call(
        functools.partial(forward_kernel, tick),
        grid_spec=grid_spec,
        out_shape=[shaped(ROWS, PAY)] + [shaped(*v.shape, dtype=v.dtype) for v in (g_buf, z_buf, h_buf)],
        input_output_aliases={9: 1, 10: 2, 11: 3},
        compiler_params=PARAMS,
        name="forward_stage",
    )(scalars, *payloads, rows, cot, w, ab, g_buf, z_buf, h_buf)


def backward_tick(tick, scalars, payloads, last_in, wt, ab, g_buf, z_buf, q_buf, zr_buf, e_buf):
    grid_spec = pltpu.PrefetchScalarGridSpec(
        num_scalar_prefetch=1,
        grid=(1,),
        in_specs=[IN_VMEM] * 10 + [slot_spec(backward_block, tick, columns) for columns in (WIDE, RANK)]
        + [ANYWHERE] * 3,
        out_specs=[IN_VMEM] * 2 + [slot_spec(backward_save, tick, columns) for columns in (RANK, RANK, CHUNK)],
    )
    return pl.pallas_call(
        functools.partial(backward_kernel, tick),
        grid_spec=grid_spec,
        out_shape=[shaped(ROWS, PAY_EXTRA), shaped(ROWS, PAY)]
        + [shaped(*v.shape, dtype=v.dtype) for v in (q_buf, zr_buf, e_buf)],
        input_output_aliases={13: 2, 14: 3, 15: 4},
        compiler_params=PARAMS,
        name="backward_stage",
    )(scalars, *payloads, *last_in, wt, ab, g_buf, z_buf, q_buf, zr_buf, e_buf)


def gradients(scalars, x_in, h_buf, q_buf, zr_buf, e_buf):
    flat = lambda v: v.reshape(-1, v.shape[-1])
    whole = lambda columns: pl.BlockSpec((TOKENS, columns), lambda i, sc: (0, 0))
    grid_spec = pltpu.PrefetchScalarGridSpec(
        num_scalar_prefetch=1,
        grid=(LAYERS // STYLES_AT_ONCE,),
        in_specs=[whole(CHUNK), whole(CHUNK), whole(RANK), whole(RANK), whole(CHUNK)],
        out_specs=[pl.BlockSpec((STYLES_AT_ONCE, 1, CHUNK, RANK), lambda i, sc: (i, 0, 0, 0)),
                   pl.BlockSpec((STYLES_AT_ONCE, 1, RANK, CHUNK), lambda i, sc: (i, 0, 0, 0))],
        scratch_shapes=[pltpu.VMEM((CHUNK, TOKENS), BF), pltpu.VMEM((RANK, TOKENS), BF)],
    )
    return pl.pallas_call(
        gradient_kernel,
        grid_spec=grid_spec,
        out_shape=[shaped(LAYERS, 1, CHUNK, RANK), shaped(LAYERS, 1, RANK, CHUNK)],
        compiler_params=PARAMS,
        name="style_gradients",
    )(scalars, x_in, flat(h_buf), flat(q_buf), flat(zr_buf), flat(e_buf))


def body(x_in, cotangent, weights, down_weight_store, lib_b, style_ids, slot_of):
    section = lax.axis_index("section")
    tp = lax.axis_index("tp")
    core, z_pos, y_pos = section % 2, tp // SIDE, tp % SIDE
    a = jnp.where(core == 0, y_pos, z_pos)
    b = jnp.where(core == 0, z_pos, y_pos)
    flat_ids = style_ids.reshape(-1)
    styles = jnp.arange(slot_of.shape[0], dtype=jnp.int32)
    slots = jnp.sum(jnp.where(flat_ids[:, None] == styles[None, :], slot_of[None, :], 0), axis=1)
    place = jnp.stack([core, section, a, b, 0, 0, 0, 0]).astype(jnp.int32)
    scalars = jnp.concatenate([place, slots, flat_ids])

    with jax.named_scope("weight_blocks"):
        cut = copy_kernel("cut_weights", cut_weights_kernel, SIDE * SIDE, [shaped(SIDE, CHUNK, CHUNK)] * SIDE, ANYWHERE,
                          place, weights[0].reshape(SIDE * SIDE, CHUNK, CHUNK))
        cut = [piece.reshape(WIDE, CHUNK) for piece in cut]
        w_pieces = [cut[0]] + [send(cut[k], along_a(k)) for k in range(1, SIDE)]
        w_prev_first = send(transposed(cut[0][None], 0, 1), onward(0))
    with jax.named_scope("adapters"):
        down, up, _ = lax.optimization_barrier((down_weight_store, lib_b, cut[0]))
        ab_out = pack_layers(down, up)
        ab_in = lax.all_to_all(ab_out, "section", split_axis=0, concat_axis=0, tiled=True)
    with jax.named_scope("blocks"):
        first, second = copy_kernel(
            "pack_blocks", pack_blocks_kernel, 1 + BLOCKS,
            [shaped(TOKENS + FIRST_BLOCKS * PAIR, CHUNK), shaped((BLOCKS - FIRST_BLOCKS) * PAIR, CHUNK)], ANYWHERE,
            scalars, x_in, ab_in)
        first_below, second_above = send(first, along_b(1)), send(second, along_b(3))
        second_below, first_above = send(second, along_b(1)), send(first, along_b(3))
        first_far, second_far = send(first_below, along_b(1)), send(second_above, along_b(3))
        block_pieces = [first, second, first_below, second_below, first_far, second_far, first_above, second_above]
    with jax.named_scope("weight_blocks"):
        w_pieces[0], w_prev_first = lax.optimization_barrier((w_pieces[0], w_prev_first))
        w_own = settle_weights(place, w_pieces)
        w_turned = transposed(w_own, 1, SIDE)
    with jax.named_scope("previous_weights"):
        w_prev = send(w_turned, onward(0))
    with jax.named_scope("blocks"):
        block_pieces[0], _ = lax.optimization_barrier((block_pieces[0], w_turned))
        x_rows, ab = settle_blocks(place, block_pieces)

    first_in = jnp.zeros((ROWS, PAY), BF)
    fwd_in = [first_in] * SIDE
    bwd_in = [jnp.zeros((ROWS, PAY_EXTRA), BF)] + [jnp.zeros((ROWS, PAY), BF)] * (SIDE - 1)
    buffer = lambda columns, dtype: jnp.zeros((BLOCKS + 1, ROWS, columns), dtype)
    g_buf, z_buf, h_buf = buffer(WIDE, F32), buffer(RANK, BF), buffer(CHUNK, BF)
    q_buf, zr_buf, e_buf = buffer(RANK, BF), buffer(RANK, BF), buffer(CHUNK, BF)
    for tick in range(2 * LAYERS + BLOCKS):
        if tick == 4:
            with jax.named_scope("previous_weights"):
                w_prev, fwd_in[0] = lax.optimization_barrier((w_prev, fwd_in[0]))
                w_prev = copy_kernel("settle_previous", settle_previous_kernel, SIDE, shaped(SIDE, CHUNK, WIDE),
                                     IN_VMEM, place, w_prev_first, w_prev)
        if tick < LAYERS + BLOCKS:
            with jax.named_scope("forward"):
                last_in = fwd_in
                pay, g_buf, z_buf, h_buf = forward_tick(
                    tick, place, fwd_in, x_rows, cotangent, w_own, ab, g_buf, z_buf, h_buf)
                if tick < LAYERS + BLOCKS - 1:
                    fwd_in = [send(pay, onward(k)) for k in range(SIDE)]
        if tick >= LAYERS:
            with jax.named_scope("backward"):
                pay0, pay, q_buf, zr_buf, e_buf = backward_tick(
                    tick, place, bwd_in, last_in, w_prev, ab, g_buf, z_buf, q_buf, zr_buf, e_buf)
                if tick < 2 * LAYERS + BLOCKS - 1:
                    bwd_in = [send(pay0, backward(0))] + [send(pay, backward(k)) for k in range(1, SIDE)]
    with jax.named_scope("gradients"):
        grad_a, grad_b = gradients(scalars, x_in, h_buf, q_buf, zr_buf, e_buf)
    return grad_a, grad_b


def solution(mesh):
    in_specs = (
        P(None, "tp"),
        P(None, "tp"),
        P("section", None, "tp"),
        P("section", None, "tp", None),
        P("section", None, None, "tp"),
        P(),
        P(),
    )
    out_specs = (P(None, "section", "tp", None), P(None, "section", None, "tp"))
    return jax.shard_map(body, mesh=mesh, in_specs=in_specs, out_specs=out_specs, check_vma=False)
```

```python
import functools

import jax
import jax.numpy as jnp
from jax import lax
from jax.experimental import pallas as pl
from jax.experimental.pallas import tpu as pltpu
from jax.sharding import PartitionSpec as P

ADAPTER_SCALE = 0.25
SIDE = 4
LAYERS = 8
BLOCKS = 8
ROWS = 32
TOKENS = BLOCKS * ROWS
RANK = 128
CHUNK = 384
WIDE = SIDE * CHUNK
PARTS = CHUNK // RANK
PAIR = 2 * RANK
FIRST_BLOCKS = 4
LAST_FORWARD = LAYERS + BLOCKS - 1
LAST_BACKWARD = 2 * LAYERS + BLOCKS - 1
Z_AT = WIDE
OWN_AT = WIDE + RANK
PAY = OWN_AT + CHUNK
PAY_EXTRA = PAY + RANK + CHUNK
STYLES_AT_ONCE = 4
BF = jnp.bfloat16
F32 = jnp.float32


def along_a(k):
    return lambda x, c, z, y: (x, c, z, y + k) if c == 0 else (x, c, z + k, y)


def along_b(k):
    return lambda x, c, z, y: (x, c, z + k, y) if c == 0 else (x, c, z, y + k)


def onward(k):
    return lambda x, c, z, y: (x, 1, z, y + k) if c == 0 else (x + 1, 0, z + k, y)


def backward(k):
    return lambda x, c, z, y: (x, 0, z + k, y) if c == 1 else (x - 1, 1, z, y + k)


def send(value, target):
    pairs = []
    for sec in range(2 * SIDE):
        for tp in range(SIDE * SIDE):
            x, c, z, y = target(sec // 2, sec % 2, tp // SIDE, tp % SIDE)
            sec_to = (x % SIDE) * 2 + c
            tp_to = (z % SIDE) * SIDE + y % SIDE
            pairs.append((sec * SIDE * SIDE + tp, sec_to * SIDE * SIDE + tp_to))
    return lax.ppermute(value, ("section", "tp"), pairs)


IN_VMEM = pl.BlockSpec(memory_space=pltpu.VMEM)
IN_SMEM = pl.BlockSpec(memory_space=pltpu.SMEM)
ANYWHERE = pl.BlockSpec(memory_space=pl.ANY)
SMALL = pl.CostEstimate(flops=0, bytes_accessed=1024, transcendentals=0)
PARAMS = pltpu.CompilerParams(vmem_limit_bytes=16 << 20)


def shaped(*shape, dtype=BF):
    return jax.ShapeDtypeStruct(shape, dtype)


def chunk_at(index):
    return pl.ds(pl.multiple_of(index * CHUNK, CHUNK), CHUNK)


def dot(left, right):
    return jnp.dot(left, right, preferred_element_type=F32)


def dot_nt(left, right):
    return lax.dot_general(left, right, (((1,), (1,)), ((), ())), preferred_element_type=F32)


def dot_tn(left, right):
    return lax.dot_general(left, right, (((0,), (0,)), ((), ())), preferred_element_type=F32)


def parts(value):
    return [value[:, part * RANK:(part + 1) * RANK] for part in range(PARTS)]


def gelu_both(y):
    scale = 0.7978845608028654
    square = y * y
    t = jnp.tanh(scale * y * (1.0 + 0.044715 * square))
    half = 0.5 * (1.0 + t)
    slope = half + 0.5 * y * (1.0 - t * t) * scale * (1.0 + 3.0 * 0.044715 * square)
    return y * half, slope


def run_copies(moves, sems):
    copies = [pltpu.make_async_copy(source, target, sems.at[i]) for i, (source, target) in enumerate(moves)]
    for copy in copies:
        copy.start()
    for copy in copies:
        copy.wait()


def copy_kernel(name, kernel, count, out_shape, out_spec, scalars, *operands):
    many = isinstance(out_shape, list)
    return pl.pallas_call(
        kernel,
        in_specs=[IN_SMEM] + [ANYWHERE] * len(operands),
        out_specs=[out_spec] * len(out_shape) if many else out_spec,
        out_shape=out_shape,
        scratch_shapes=[pltpu.SemaphoreType.DMA((count,))],
        compiler_params=PARAMS,
        cost_estimate=SMALL,
        name=name,
    )(scalars, *operands)


def pack_layers_kernel(a, b, out):
    for layer in range(LAYERS):
        for part in range(PARTS):
            out[layer, :RANK, part * RANK:(part + 1) * RANK] = a[0, layer, part * RANK:(part + 1) * RANK]
        out[layer, RANK:] = b[0, (layer - 1) % LAYERS]


def pack_layers(a, b):
    return pl.pallas_call(
        pack_layers_kernel,
        in_specs=[IN_VMEM] * 2,
        out_specs=IN_VMEM,
        out_shape=shaped(LAYERS, PAIR, CHUNK),
        compiler_params=PARAMS,
        name="pack_layers",
    )(a, b)


def cut_weights_kernel(sc, w, o0, o1, o2, o3, sems):
    core, a = sc[0], sc[2]
    moves = []
    for k, out in enumerate((o0, o1, o2, o3)):
        to = lax.rem(a + k, SIDE)
        for j in range(SIDE):
            source = jnp.where(core == 0, j * SIDE + to, to * SIDE + j)
            moves.append((w.at[source], out.at[j]))
    run_copies(moves, sems)


def pack_blocks_kernel(sc, x, ab, first, second, sems):
    moves = [(x, first.at[pl.ds(0, TOKENS)])]
    for n in range(BLOCKS):
        out, start = (first, TOKENS + n * PAIR) if n < FIRST_BLOCKS else (second, (n - FIRST_BLOCKS) * PAIR)
        moves.append((ab.at[sc[8 + n]], out.at[pl.ds(start, PAIR)]))
    run_copies(moves, sems)


def settle_weights_kernel(sc, own, w1, w2, w3, out, sems):
    copies = [pltpu.make_async_copy(w, out.at[k + 1], sems.at[k]) for k, w in enumerate((w1, w2, w3))]
    for copy in copies:
        copy.start()
    out[0] = own[...]
    for copy in copies:
        copy.wait()


def settle_weights(scalars, pieces):
    return pl.pallas_call(
        settle_weights_kernel,
        in_specs=[IN_SMEM, IN_VMEM] + [ANYWHERE] * (SIDE - 1),
        out_specs=IN_VMEM,
        out_shape=shaped(SIDE, WIDE, CHUNK),
        scratch_shapes=[pltpu.SemaphoreType.DMA((SIDE - 1,))],
        compiler_params=PARAMS,
        cost_estimate=SMALL,
        name="settle_weights",
    )(scalars, *pieces)


def settle_blocks_kernel(sc, f0, s0, f1, s1, f2, s2, f3, s3, x, ab, sems):
    early, late = pl.ds(0, FIRST_BLOCKS * PAIR), pl.ds(FIRST_BLOCKS * PAIR, (BLOCKS - FIRST_BLOCKS) * PAIR)
    head, tail = pl.ds(0, TOKENS), pl.ds(TOKENS, FIRST_BLOCKS * PAIR)
    copies = []
    for k, (first, second) in ((1, (f1, s1)), (2, (f2, s2)), (3, (f3, s3))):
        for i, (source, target) in enumerate((
                (first.at[head], x.at[k]), (first.at[tail], ab.at[k, early]), (second, ab.at[k, late]))):
            copies.append(pltpu.make_async_copy(source, target, sems.at[k - 1, i]))
    for copy in copies:
        copy.start()
    x[0] = f0[head]
    ab[0, early] = f0[tail]
    ab[0, late] = s0[...]
    for copy in copies:
        copy.wait()


def settle_blocks(scalars, pieces):
    return pl.pallas_call(
        settle_blocks_kernel,
        in_specs=[IN_SMEM, IN_VMEM, IN_VMEM] + [ANYWHERE] * 6,
        out_specs=[IN_VMEM] * 2,
        out_shape=[shaped(SIDE, TOKENS, CHUNK), shaped(SIDE, BLOCKS * PAIR, CHUNK)],
        scratch_shapes=[pltpu.SemaphoreType.DMA((SIDE - 1, 3))],
        compiler_params=PARAMS,
        cost_estimate=SMALL,
        name="settle_blocks",
    )(scalars, *pieces)


def settle_previous_kernel(sc, first, rest, out, sems):
    run_copies([(first.at[0], out.at[0])] + [(rest.at[k - 1], out.at[k]) for k in range(1, SIDE)], sems)


def transpose_kernel(w, out):
    out[0] = w[0].T


def transposed(w, begin, end):
    return pl.pallas_call(
        transpose_kernel,
        grid=(end - begin,),
        in_specs=[pl.BlockSpec((1, WIDE, CHUNK), lambda i: (i + begin, 0, 0))],
        out_specs=pl.BlockSpec((1, CHUNK, WIDE), lambda i: (i, 0, 0)),
        out_shape=shaped(end - begin, CHUNK, WIDE),
        compiler_params=PARAMS,
        cost_estimate=SMALL,
        name="transpose_weights",
    )(w)


def within(index):
    return jnp.clip(index, 0, BLOCKS - 1)


def slot_or_spare(index):
    return jnp.where((index >= 0) & (index < BLOCKS), index, BLOCKS)


def forward_block(tick, section):
    return within(tick - jnp.where((section == 0) & (tick >= LAYERS), LAYERS, section))


def boundary(section):
    return jnp.where(section == 0, LAYERS, section)


def forward_save(tick, section):
    return slot_or_spare(tick - boundary(section))


def backward_block(tick, section):
    return within(tick - 2 * LAYERS + boundary(section))


def backward_save(tick, section):
    return slot_or_spare(tick - 2 * LAYERS + section)


def forward_kernel(tick, sc, p0, p1, p2, p3, rows, cot, w, ab, _g, _z, _h, pay, g_out, z_out, h_out, h_all):
    section, a, b = sc[1], sc[2], sc[3]
    block = forward_block(tick, section)
    own_rows = pl.ds(pl.multiple_of(block * ROWS, ROWS), ROWS)
    down = pl.ds(pl.multiple_of(block * PAIR, PAIR), RANK)
    up = pl.ds(pl.multiple_of(block * PAIR + RANK, RANK), RANK)
    z = sum(p[:, Z_AT:OWN_AT].astype(F32) for p in (p0, p1, p2, p3)).astype(BF)
    z_out[0] = z
    z_part = jnp.zeros((ROWS, RANK), F32)
    for k, p in enumerate((p0, p1, p2, p3)):
        here = chunk_at(lax.rem(b - k + SIDE, SIDE))
        y = sum(q[:, here].astype(F32) for q in (p0, p1, p2, p3))
        value, slope = gelu_both(y + ADAPTER_SCALE * dot(z, ab[k, up]))
        h = (p[:, OWN_AT:PAY].astype(F32) + value).astype(BF)
        if tick < LAYERS:
            h = jnp.where(section == 0, rows[k, own_rows], h)
        h_all[:, here] = h
        g_out[0, :, here] = slope
        if tick < LAST_FORWARD:
            for piece, weight in zip(parts(h), parts(ab[k, down])):
                z_part = z_part + dot(piece, weight)
        if k == 0:
            h_out[0] = h
            pay[:, OWN_AT:PAY] = jnp.where(section == LAYERS - 1, cot[own_rows], h)
    pay[:, Z_AT:OWN_AT] = z_part.astype(BF)
    if tick == LAST_FORWARD:
        return
    h = h_all[...]
    for k in range(SIDE):
        pay[:, chunk_at(lax.rem(a - k + SIDE, SIDE))] = dot(h, w[k]).astype(BF)


def backward_kernel(tick, sc, q0, q1, q2, q3, p0, p1, p2, p3, wt, ab, slope, z_in,
                    _q, _z, _e, pay0, pay, q_out, z_out, e_out):
    section, b = sc[1], sc[3]
    block = backward_block(tick, section)
    short = tick == LAST_BACKWARD
    z_at, extra = (0, RANK) if short else (Z_AT, PAY)
    q = sum(p[:, z_at:z_at + RANK].astype(F32) for p in (q0, q1, q2, q3)).astype(BF)
    q_out[0] = q
    z_out[0] = q0[:, extra:extra + RANK]
    e_out[0] = q0[:, extra + RANK:]
    if short:
        return
    closing = tick == LAST_BACKWARD - 1
    q_part = jnp.zeros((ROWS, RANK), F32)
    total = jnp.zeros((ROWS, WIDE), F32)
    down = pl.ds(pl.multiple_of(block * PAIR, PAIR), RANK)
    up = pl.ds(pl.multiple_of(block * PAIR + RANK, RANK), RANK)
    for k, (p, cot) in enumerate(((q0, p0), (q1, p1), (q2, p2), (q3, p3))):
        here = chunk_at(lax.rem(b - k + SIDE, SIDE))
        n = sum(r[:, here].astype(F32) for r in (q0, q1, q2, q3))
        back = jnp.concatenate([dot_nt(q, weight) for weight in parts(ab[k, down])], axis=1)
        g = (p[:, OWN_AT:PAY].astype(F32) + n + back).astype(BF)
        if tick <= LAST_FORWARD:
            g = jnp.where(section == 0, cot[:, OWN_AT:PAY], g)
        e = (slope[0, :, here] * g.astype(F32)).astype(BF)
        q_part = q_part + dot_nt(e, ab[k, up])
        if closing:
            if k == 0:
                pay0[:, 2 * RANK:] = e
            continue
        total = total + dot(e, wt[k])
        if k == 0:
            pay[:, OWN_AT:PAY] = g
            pay0[:, OWN_AT:PAY] = g
            pay0[:, PAY + RANK:] = e
    q_part = (ADAPTER_SCALE * q_part).astype(BF)
    if closing:
        pay[...] = q_part
        pay0[:, :RANK] = q_part
        pay0[:, RANK:2 * RANK] = z_in[0]
        return
    pay[:, Z_AT:OWN_AT] = q_part
    pay0[:, Z_AT:OWN_AT] = q_part
    pay0[:, PAY:PAY + RANK] = z_in[0]
    n = total.astype(BF)
    pay[:, :WIDE] = n
    pay0[:, :WIDE] = n


def gradient_kernel(sc, x, h, q, z, e, ga, gb, h_turned, z_turned):
    @pl.when(pl.program_id(0) == 0)
    def _():
        h_turned[...] = jnp.where(sc[1] == 0, x[...], h[...]).T
        z_turned[...] = z[...].T

    block = lax.broadcasted_iota(jnp.int32, (1, TOKENS), 1) // ROWS
    for i in range(STYLES_AT_ONCE):
        style = pl.program_id(0) * STYLES_AT_ONCE + i
        keep = jnp.zeros((1, TOKENS), F32)
        for n in range(BLOCKS):
            keep = jnp.where((block == n) & (sc[16 + n] == style), 1.0, keep)
        keep = keep.astype(BF)
        ga[i, 0] = dot(h_turned[...] * keep, q[...]).astype(BF)
        gb[i, 0] = (ADAPTER_SCALE * dot(z_turned[...] * keep, e[...])).astype(BF)


def slot_spec(slot, tick, columns):
    return pl.BlockSpec((1, ROWS, columns), lambda i, sc: (slot(tick, sc[1]), 0, 0))


def forward_tick(tick, scalars, payloads, rows, cot, w, ab, g_buf, z_buf, h_buf):
    grid_spec = pltpu.PrefetchScalarGridSpec(
        num_scalar_prefetch=1,
        grid=(1,),
        in_specs=[IN_VMEM] * 8 + [ANYWHERE] * 3,
        out_specs=[IN_VMEM] + [slot_spec(forward_save, tick, columns) for columns in (WIDE, RANK, CHUNK)],
        scratch_shapes=[pltpu.VMEM((ROWS, WIDE), BF)],
    )
    return pl.pallas_call(
        functools.partial(forward_kernel, tick),
        grid_spec=grid_spec,
        out_shape=[shaped(ROWS, PAY)] + [shaped(*v.shape, dtype=v.dtype) for v in (g_buf, z_buf, h_buf)],
        input_output_aliases={9: 1, 10: 2, 11: 3},
        compiler_params=PARAMS,
        name="forward_stage",
    )(scalars, *payloads, rows, cot, w, ab, g_buf, z_buf, h_buf)


def backward_tick(tick, scalars, payloads, last_in, wt, ab, g_buf, z_buf, q_buf, zr_buf, e_buf):
    columns0, columns = (2 * RANK + CHUNK, RANK) if tick >= LAST_BACKWARD - 1 else (PAY_EXTRA, PAY)
    grid_spec = pltpu.PrefetchScalarGridSpec(
        num_scalar_prefetch=1,
        grid=(1,),
        in_specs=[IN_VMEM] * 10 + [slot_spec(backward_block, tick, width) for width in (WIDE, RANK)]
        + [ANYWHERE] * 3,
        out_specs=[IN_VMEM] * 2 + [slot_spec(backward_save, tick, width) for width in (RANK, RANK, CHUNK)],
    )
    return pl.pallas_call(
        functools.partial(backward_kernel, tick),
        grid_spec=grid_spec,
        out_shape=[shaped(ROWS, columns0), shaped(ROWS, columns)]
        + [shaped(*v.shape, dtype=v.dtype) for v in (q_buf, zr_buf, e_buf)],
        input_output_aliases={13: 2, 14: 3, 15: 4},
        compiler_params=PARAMS,
        name="backward_stage",
    )(scalars, *payloads, *last_in, wt, ab, g_buf, z_buf, q_buf, zr_buf, e_buf)


def gradients(scalars, x_in, h_buf, q_buf, zr_buf, e_buf):
    flat = lambda v: v.reshape(-1, v.shape[-1])
    whole = lambda columns: pl.BlockSpec((TOKENS, columns), lambda i, sc: (0, 0))
    grid_spec = pltpu.PrefetchScalarGridSpec(
        num_scalar_prefetch=1,
        grid=(LAYERS // STYLES_AT_ONCE,),
        in_specs=[whole(CHUNK), whole(CHUNK), whole(RANK), whole(RANK), whole(CHUNK)],
        out_specs=[pl.BlockSpec((STYLES_AT_ONCE, 1, CHUNK, RANK), lambda i, sc: (i, 0, 0, 0)),
                   pl.BlockSpec((STYLES_AT_ONCE, 1, RANK, CHUNK), lambda i, sc: (i, 0, 0, 0))],
        scratch_shapes=[pltpu.VMEM((CHUNK, TOKENS), BF), pltpu.VMEM((RANK, TOKENS), BF)],
    )
    return pl.pallas_call(
        gradient_kernel,
        grid_spec=grid_spec,
        out_shape=[shaped(LAYERS, 1, CHUNK, RANK), shaped(LAYERS, 1, RANK, CHUNK)],
        compiler_params=PARAMS,
        name="style_gradients",
    )(scalars, x_in, flat(h_buf), flat(q_buf), flat(zr_buf), flat(e_buf))


def body(x_in, cotangent, weights, down_weight_store, lib_b, style_ids, slot_of):
    section = lax.axis_index("section")
    tp = lax.axis_index("tp")
    core, z_pos, y_pos = section % 2, tp // SIDE, tp % SIDE
    a = jnp.where(core == 0, y_pos, z_pos)
    b = jnp.where(core == 0, z_pos, y_pos)
    flat_ids = style_ids.reshape(-1)
    styles = jnp.arange(slot_of.shape[0], dtype=jnp.int32)
    slots = jnp.sum(jnp.where(flat_ids[:, None] == styles[None, :], slot_of[None, :], 0), axis=1)
    place = jnp.stack([core, section, a, b, 0, 0, 0, 0]).astype(jnp.int32)
    scalars = jnp.concatenate([place, slots, flat_ids])

    with jax.named_scope("weight_blocks"):
        cut = copy_kernel("cut_weights", cut_weights_kernel, SIDE * SIDE, [shaped(SIDE, CHUNK, CHUNK)] * SIDE, ANYWHERE,
                          place, weights[0].reshape(SIDE * SIDE, CHUNK, CHUNK))
        cut = [piece.reshape(WIDE, CHUNK) for piece in cut]
        w_pieces = [cut[0]] + [send(cut[k], along_a(k)) for k in range(1, SIDE)]
        w_prev_first = send(transposed(cut[0][None], 0, 1), onward(0))
    with jax.named_scope("adapters"):
        down, up, _ = lax.optimization_barrier((down_weight_store, lib_b, cut[0]))
        ab_out = pack_layers(down, up)
        ab_in = lax.all_to_all(ab_out, "section", split_axis=0, concat_axis=0, tiled=True)
    with jax.named_scope("blocks"):
        first, second = copy_kernel(
            "pack_blocks", pack_blocks_kernel, 1 + BLOCKS,
            [shaped(TOKENS + FIRST_BLOCKS * PAIR, CHUNK), shaped((BLOCKS - FIRST_BLOCKS) * PAIR, CHUNK)], ANYWHERE,
            scalars, x_in, ab_in)
        first_below, second_above = send(first, along_b(1)), send(second, along_b(3))
        second_below, first_above = send(second, along_b(1)), send(first, along_b(3))
        first_far, second_far = send(first_below, along_b(1)), send(second_above, along_b(3))
        block_pieces = [first, second, first_below, second_below, first_far, second_far, first_above, second_above]
    with jax.named_scope("weight_blocks"):
        w_pieces[0], w_prev_first = lax.optimization_barrier((w_pieces[0], w_prev_first))
        w_own = settle_weights(place, w_pieces)
        w_turned = transposed(w_own, 1, SIDE)
    with jax.named_scope("previous_weights"):
        w_prev = send(w_turned, onward(0))
    with jax.named_scope("blocks"):
        block_pieces[0], _ = lax.optimization_barrier((block_pieces[0], w_turned))
        x_rows, ab = settle_blocks(place, block_pieces)

    first_in = jnp.zeros((ROWS, PAY), BF)
    fwd_in = [first_in] * SIDE
    bwd_in = [jnp.zeros((ROWS, PAY_EXTRA), BF)] + [jnp.zeros((ROWS, PAY), BF)] * (SIDE - 1)
    buffer = lambda columns, dtype: jnp.zeros((BLOCKS + 1, ROWS, columns), dtype)
    g_buf, z_buf, h_buf = buffer(WIDE, F32), buffer(RANK, BF), buffer(CHUNK, BF)
    q_buf, zr_buf, e_buf = buffer(RANK, BF), buffer(RANK, BF), buffer(CHUNK, BF)
    for tick in range(2 * LAYERS + BLOCKS):
        if tick == 4:
            with jax.named_scope("previous_weights"):
                w_prev, fwd_in[0] = lax.optimization_barrier((w_prev, fwd_in[0]))
                w_prev = copy_kernel("settle_previous", settle_previous_kernel, SIDE, shaped(SIDE, CHUNK, WIDE),
                                     IN_VMEM, place, w_prev_first, w_prev)
        if tick < LAYERS + BLOCKS:
            with jax.named_scope("forward"):
                last_in = fwd_in
                pay, g_buf, z_buf, h_buf = forward_tick(
                    tick, place, fwd_in, x_rows, cotangent, w_own, ab, g_buf, z_buf, h_buf)
                if tick < LAYERS + BLOCKS - 1:
                    fwd_in = [send(pay, onward(k)) for k in range(SIDE)]
        if tick >= LAYERS:
            with jax.named_scope("backward"):
                pay0, pay, q_buf, zr_buf, e_buf = backward_tick(
                    tick, place, bwd_in, last_in, w_prev, ab, g_buf, z_buf, q_buf, zr_buf, e_buf)
                if tick < 2 * LAYERS + BLOCKS - 1:
                    bwd_in = [send(pay0, backward(0))] + [send(pay, backward(k)) for k in range(1, SIDE)]
    with jax.named_scope("gradients"):
        grad_a, grad_b = gradients(scalars, x_in, h_buf, q_buf, zr_buf, e_buf)
    return grad_a, grad_b


def solution(mesh):
    in_specs = (
        P(None, "tp"),
        P(None, "tp"),
        P("section", None, "tp"),
        P("section", None, "tp", None),
        P("section", None, None, "tp"),
        P(),
        P(),
    )
    out_specs = (P(None, "section", "tp", None), P(None, "section", None, "tp"))
    return jax.shard_map(body, mesh=mesh, in_specs=in_specs, out_specs=out_specs, check_vma=False)
```
